32 devices in a mesh: seq: 8 (over z, y), head: 4 (over x, core).
Axes of the slice: x: 2, y: 2, z: 4, core: 2. Of those that a mesh axis runs over, the one named last changes fastest.
Arguments:
- query: bfloat16 [2048, 512], P('seq', 'head'), may hold values from -131 to 131
- keys: bfloat16 [2048, 512], P('seq', 'head'), may hold values from -5 to 5, as said below
- values: bfloat16 [2048, 512], P('seq', 'head'), may hold values from -5 to 5, as said below
- d_out: bfloat16 [2048, 5376], P('seq', 'head'), may hold values from -6 to 6
- w_out: bfloat16 [512, 5376], P('head'), may hold values from -0.25 to 0.25
- w_query: bfloat16 [5376, 512], P(None, 'head'), may hold values from -0.078125 to 0.078125
- w_key: bfloat16 [5376, 512], P(None, 'head'), as said below
- w_value: bfloat16 [5376, 512], P(None, 'head'), as said below
Outputs:
- grad_input: bfloat16 [2048, 5376], P('seq', 'head')
The draws below stay inside these ranges and needn't reach their ends.
Inputs may be any that keep to these rules, and one draw needn't show every extreme that they name: `keys`: the columns of query heads 2i and 2i + 1 are equal: both read key head i. `values`: the columns of query heads 2i and 2i + 1 are equal: both read value head i. `w_key`: the columns of query heads 2i and 2i + 1 are equal; every entry lies within 5 / sqrt(5376) in magnitude. `w_value`: the columns of query heads 2i and 2i + 1 are equal; every entry lies within 5 / sqrt(5376) in magnitude.
All inputs are finite; a program needn't handle non-finite values.
Results may differ from the reference program's by a relative error of at most 0.03.
Values may be sent and summed in bfloat16 or wider, within the bound.
A program may use at most 64 MiB of HBM per device.

```python
import jax
import jax.numpy as jnp
from jax import lax

D = 5376
HEAD_DIM = 128
WINDOW = 1024
TOK_DEV = 256
QHEADS = 4
KVHEADS = 2
TOKENS = 2048
NBR = 4


def shared_keys(key):
    return jax.random.truncated_normal(jax.random.fold_in(key, 101), -5.0, 5.0, (TOKENS, KVHEADS, HEAD_DIM), jnp.float32)


def paired(fields, leading):
    return jnp.repeat(fields, 2, axis=1).reshape(leading, QHEADS * HEAD_DIM).astype(jnp.bfloat16)


def draw_query(key, part):
    queries = jax.random.truncated_normal(jax.random.fold_in(key, 102), -5.0, 5.0, (TOKENS, QHEADS, HEAD_DIM), jnp.float32)
    return queries.reshape(TOKENS, QHEADS * HEAD_DIM).astype(jnp.bfloat16)


def draw_keys(key, part):
    fields = shared_keys(key)
    return paired(fields, TOKENS)


def draw_values(key, part):
    fields = jax.random.truncated_normal(jax.random.fold_in(key, 104), -5.0, 5.0, (TOKENS, KVHEADS, HEAD_DIM), jnp.float32)
    return paired(fields, TOKENS)


def draw_w_key(key, part):
    fields = jax.random.truncated_normal(jax.random.fold_in(key, 105), -5.0, 5.0, (D, KVHEADS, HEAD_DIM), jnp.float32)
    return paired(fields * D ** (-0.5), D)


def draw_w_value(key, part):
    fields = jax.random.truncated_normal(jax.random.fold_in(key, 106), -5.0, 5.0, (D, KVHEADS, HEAD_DIM), jnp.float32)
    return paired(fields * D ** (-0.5), D)


def block_scale(key, shape, pieces, low, high):
    level = 1.0
    for dim, blocks in pieces:
        draws = jax.random.uniform(jax.random.fold_in(jax.random.fold_in(key, 6), dim), (blocks,), jnp.float32, low / len(pieces), high / len(pieces))
        level = level * jnp.repeat(jnp.exp(draws), shape[dim] // blocks).reshape((-1,) + (1,) * (len(shape) - 1 - dim))
    return level


def centred(rng, extent, deviation, bound, split=(), kind=jnp.bfloat16):
    result = deviation * jax.random.normal(rng, extent, jnp.float32)
    if split:
        result = result * block_scale(rng, extent, split, -0.22, 0.18)
    return jnp.clip(result, -bound, bound).astype(kind)


def setup_inputs(seed: int = 0) -> dict:
    seeds = jax.random.split(jax.random.key(seed), 9)
    query = draw_query(jax.random.fold_in(seeds[8], 71), 0)
    keys = draw_keys(jax.random.fold_in(seeds[8], 71), 0)
    values = draw_values(jax.random.fold_in(seeds[8], 71), 0)
    d_out = centred(seeds[3], (TOKENS, D), 1.0, 6.0, ((0, 8), (1, 4)))
    w_out = centred(seeds[4], (QHEADS * HEAD_DIM, D), (QHEADS * HEAD_DIM) ** -0.5, 0.25, ((0, 4),))
    w_query = centred(seeds[5], (D, QHEADS * HEAD_DIM), D ** -0.5, 0.078125, ((1, 4),))
    w_key = draw_w_key(jax.random.fold_in(seeds[8], 71), 0)
    w_value = draw_w_value(jax.random.fold_in(seeds[8], 71), 0)
    return {"query": query, "keys": keys, "values": values, "d_out": d_out, "w_out": w_out, "w_query": w_query, "w_key": w_key, "w_value": w_value}


score_scale = 168.0 ** -0.5


def dot_rows(left, right):
    return lax.dot_general(left, right, (((1,), (1,)), ((), ())), preferred_element_type=jnp.float32)


def dot_cols(left, right):
    return lax.dot_general(left, right, (((0,), (0,)), ((), ())), preferred_element_type=jnp.float32)


def band_backward(query_block, key_band, value_band, grad_block, query_start, key_start):
    length = query_block.shape[0]
    span = key_band.shape[0]
    query_pos = query_start + jnp.arange(length, dtype=jnp.int32)
    key_pos = key_start + jnp.arange(span, dtype=jnp.int32)
    offset = query_pos[:, None] - key_pos[None, :]
    allowed = (key_pos[None, :] >= 0) & (offset >= 0) & (offset < WINDOW)
    scores = dot_rows(query_block, key_band) * score_scale
    masked = jnp.where(allowed, scores, -1e30)
    top = jnp.max(masked, axis=1, keepdims=True)
    weights = jnp.where(allowed, jnp.exp(masked - top), 0.0)
    probs = weights / jnp.sum(weights, axis=1, keepdims=True)
    probs_low = probs.astype(jnp.bfloat16)
    grad_probs = dot_rows(grad_block, value_band)
    delta = jnp.sum(probs * grad_probs, axis=1, keepdims=True)
    grad_scores = (probs * (grad_probs - delta)).astype(jnp.bfloat16)
    grad_query = (jnp.dot(grad_scores, key_band, preferred_element_type=jnp.float32) * score_scale).astype(jnp.bfloat16)
    grad_keys = (dot_cols(grad_scores, query_block) * score_scale).astype(jnp.bfloat16)
    grad_values = dot_cols(probs_low, grad_block).astype(jnp.bfloat16)
    return grad_query, grad_keys, grad_values


def head_grads(query_head, keys_head, values_head, grad_head):
    reach = NBR
    span = (reach + 1) * TOK_DEV
    blocks = TOKENS // TOK_DEV
    padding = jnp.zeros((reach * TOK_DEV, HEAD_DIM), keys_head.dtype)
    key_padded = jnp.concatenate([padding, keys_head], axis=0)
    value_padded = jnp.concatenate([padding, values_head], axis=0)

    def one_block(index):
        start = index * TOK_DEV
        query_block = lax.dynamic_slice_in_dim(query_head, start, TOK_DEV, 0)
        grad_block = lax.dynamic_slice_in_dim(grad_head, start, TOK_DEV, 0)
        key_band = lax.dynamic_slice_in_dim(key_padded, start, span, 0)
        value_band = lax.dynamic_slice_in_dim(value_padded, start, span, 0)
        return band_backward(query_block, key_band, value_band, grad_block, start, start - reach * TOK_DEV)

    grad_query, key_parts, value_parts = lax.map(one_block, jnp.arange(blocks, dtype=jnp.int32))
    grad_query = grad_query.reshape(TOKENS, HEAD_DIM)

    def assemble(parts):
        parts = parts.reshape(blocks, reach + 1, TOK_DEV, HEAD_DIM).astype(jnp.float32)
        summed = jnp.zeros(((blocks + reach) * TOK_DEV, HEAD_DIM), jnp.float32)
        for offset in range(reach + 1):
            piece = parts[:, offset].reshape(TOKENS, HEAD_DIM)
            summed = summed + jnp.pad(piece, ((offset * TOK_DEV, (reach - offset) * TOK_DEV), (0, 0)))
        return summed[reach * TOK_DEV:].astype(jnp.bfloat16)

    return grad_query, assemble(key_parts), assemble(value_parts)


def reference(query, keys, values, d_out, w_out, w_query, w_key, w_value):
    def one_head(carried, head):
        first = head * HEAD_DIM
        query_head = lax.dynamic_slice_in_dim(query, first, HEAD_DIM, 1)
        keys_head = lax.dynamic_slice_in_dim(keys, first, HEAD_DIM, 1)
        values_head = lax.dynamic_slice_in_dim(values, first, HEAD_DIM, 1)
        out_rows = lax.dynamic_slice_in_dim(w_out, first, HEAD_DIM, 0)
        grad_head = dot_rows(d_out, out_rows).astype(jnp.bfloat16)
        grad_query, grad_keys, grad_values = head_grads(query_head, keys_head, values_head, grad_head)
        term = dot_rows(grad_query, lax.dynamic_slice_in_dim(w_query, first, HEAD_DIM, 1))
        term = term + dot_rows(grad_keys, lax.dynamic_slice_in_dim(w_key, first, HEAD_DIM, 1))
        term = term + dot_rows(grad_values, lax.dynamic_slice_in_dim(w_value, first, HEAD_DIM, 1))
        rounded = lax.optimization_barrier(term.astype(jnp.bfloat16))
        return carried + rounded.astype(jnp.float32), None

    start_total = jnp.zeros((TOKENS, D), jnp.float32)
    summed, unused = lax.scan(one_head, start_total, jnp.arange(QHEADS, dtype=jnp.int32))
    return summed.astype(jnp.bfloat16)
```

```python
import functools

import jax
import jax.numpy as jnp
from jax import lax
from jax.experimental import pallas as pl
from jax.experimental.pallas import tpu as pltpu
from jax.sharding import PartitionSpec as P

WINDOW = 1024
NBR = 4
HEAD = 128


score_scale = 168.0 ** (-0.5)


def from_behind(block, axis, distance):
    devices = range(lax.axis_size(axis))
    route = [(i - distance, i) for i in devices if i - distance in devices]
    return lax.ppermute(block, axis, route)


def dot_rows(left, right):
    return lax.dot_general(
        left, right, (((1,), (1,)), ((), ())), preferred_element_type=jnp.float32
    )


def dot_cols(left, right):
    return lax.dot_general(
        left, right, (((0,), (0,)), ((), ())), preferred_element_type=jnp.float32
    )


def band_backward(query_block, key_band, value_band, grad_block, query_start, key_start):
    length = query_block.shape[0]
    span = key_band.shape[0]
    query_pos = query_start + jnp.arange(length, dtype=jnp.int32)
    key_pos = key_start + jnp.arange(span, dtype=jnp.int32)
    offset = query_pos[:, None] - key_pos[None, :]
    allowed = (key_pos[None, :] >= 0) & (offset >= 0) & (offset < WINDOW)
    scores = dot_rows(query_block, key_band) * score_scale
    masked = jnp.where(allowed, scores, -1e30)
    top = jnp.max(masked, axis=1, keepdims=True)
    weights = jnp.where(allowed, jnp.exp(masked - top), 0.0)
    probs = weights / jnp.sum(weights, axis=1, keepdims=True)
    probs_low = probs.astype(jnp.bfloat16)
    grad_probs = dot_rows(grad_block, value_band)
    delta = jnp.sum(probs * grad_probs, axis=1, keepdims=True)
    grad_scores = (probs * (grad_probs - delta)).astype(jnp.bfloat16)
    grad_query = (
        jnp.dot(grad_scores, key_band, preferred_element_type=jnp.float32) * score_scale
    ).astype(jnp.bfloat16)
    grad_keys = (dot_cols(grad_scores, query_block) * score_scale).astype(jnp.bfloat16)
    grad_values = dot_cols(probs_low, grad_block).astype(jnp.bfloat16)
    return (grad_query, grad_keys, grad_values)


def body(query, keys, values, d_out, w_out, w_query, w_key, w_value):
    length = query.shape[0]
    seq_index = lax.axis_index("seq")
    gathered = lax.all_gather(d_out, "head", axis=1, tiled=True)
    grad_heads = dot_rows(gathered, w_out).astype(jnp.bfloat16)
    reach = NBR
    key_blocks = []
    value_blocks = []
    for distance in range(reach, 0, -1):
        far_keys, far_values = from_behind((keys, values), "seq", distance)
        key_blocks.append(far_keys)
        value_blocks.append(far_values)
    key_band = jnp.concatenate(key_blocks + [keys], axis=0)
    value_band = jnp.concatenate(value_blocks + [values], axis=0)
    query_start = seq_index * length
    grad_query, key_parts, value_parts = band_backward(
        query, key_band, value_band, grad_heads, query_start, query_start - reach * length
    )
    key_total = key_parts[reach * length :].astype(jnp.float32)
    value_total = value_parts[reach * length :].astype(jnp.float32)
    for distance in range(1, reach + 1):
        first = (reach - distance) * length
        outgoing = (key_parts[first : first + length], value_parts[first : first + length])
        back_keys, back_values = from_behind((outgoing[0], outgoing[1]), "seq", -distance)
        key_total = key_total + back_keys.astype(jnp.float32)
        value_total = value_total + back_values.astype(jnp.float32)
    grad_keys = key_total.astype(jnp.bfloat16)
    grad_values = value_total.astype(jnp.bfloat16)
    summed = dot_rows(w_query, grad_query)
    summed = summed + dot_rows(w_key, grad_keys)
    summed = summed + dot_rows(w_value, grad_values)
    reduced = lax.psum_scatter(
        summed.astype(jnp.bfloat16), "head", scatter_dimension=0, tiled=True
    ).astype(jnp.float32)
    return reduced.T.astype(jnp.bfloat16)


PEERS = 4
SIB, ACROSS, DIAG = 1, 2, 3
ROW_CHUNKS = 4
MESH = pl.DeviceIdType.MESH

C_DOUT = 0
C_WOUT = C_DOUT + ROW_CHUNKS
C_HALO = C_WOUT + 2
C_PASS = C_HALO + NBR
C_PART = C_PASS + NBR
C_WSIB = C_PART + 1
C_WFAR = C_WSIB + 2
C_WFWD = C_WFAR + 4
C_SWAP = C_WFWD + 4
C_BACK = C_SWAP + 1
C_GRAD = C_BACK + NBR
C_END = C_GRAD + 6


def kernel(
    seqs, query, keys, values, d_out, w_out, w_query, w_key, w_value, out,
    wq_all, wkv_all, w_cut, w_own, w_sib, d_own, d_far, kv, probs, low, ds, partial, partial_in, heads,
    parts, parts_in, back, back_in, grads, weights, total,
    send, recv, local,
):
    s = lax.axis_index("seq")
    h = lax.axis_index("head")
    core = lax.rem(h, 2)
    sib = h + 1 - 2 * core
    across = lax.rem(h + 2, 4)
    diag = lax.rem(sib + 2, 4)
    y = lax.rem(s, 2)
    pair = s + 1 - 2 * y
    peers = (None, sib, across, diag)
    tokens = query.shape[0]
    width = out.shape[1]
    half = width // 2
    reach = NBR
    f32, bf16 = jnp.float32, jnp.bfloat16

    def remote(index, src, dst, seq, head):
        return pltpu.make_async_remote_copy(
            src_ref=src, dst_ref=dst, send_sem=send.at[index], recv_sem=recv.at[index],
            device_id=(seq, head), device_id_type=MESH,
        )

    load_wq = pltpu.make_async_copy(w_query, wq_all, local.at[0])
    load_wk = pltpu.make_async_copy(w_key, wkv_all, local.at[1])
    load_wv = pltpu.make_async_copy(w_value, wkv_all, local.at[1])
    load_wq.start()

    @pl.when(core == 0)
    def _():
        load_wk.start()

    @pl.when(core == 1)
    def _():
        load_wv.start()

    wide = d_own.shape[1]
    pad = jnp.zeros((HEAD, wide - width), bf16)
    d_own[...] = jnp.concatenate([d_out[...], jnp.zeros((tokens, wide - width), bf16)], axis=1)
    kv[0, reach] = keys[...]
    kv[1, reach] = values[...]
    for d in range(1, reach + 1):
        @pl.when(s < d)
        def _():
            kv[0, reach - d] = jnp.zeros((tokens, HEAD), bf16)
            kv[1, reach - d] = jnp.zeros((tokens, HEAD), bf16)

    barrier = pltpu.get_barrier_semaphore()
    for r in range(1, PEERS):
        pl.semaphore_signal(barrier, inc=1, device_id=(s, peers[r]), device_id_type=MESH)
    for d in range(1, reach + 1):
        @pl.when(s >= d)
        def _():
            pl.semaphore_signal(barrier, inc=1, device_id=(s - d, h), device_id_type=MESH)

        @pl.when(s + d < seqs)
        def _():
            pl.semaphore_signal(barrier, inc=1, device_id=(s + d, h), device_id_type=MESH)
    behind = jnp.minimum(s, reach)
    ahead = jnp.minimum(seqs - 1 - s, reach)
    pl.semaphore_wait(barrier, PEERS - 1 + behind + ahead)

    rows = tokens // ROW_CHUNKS
    dout_copies = [
        remote(C_DOUT + i, d_own.at[pl.ds(i * rows, rows)], d_far.at[pl.ds(i * rows, rows)], s, across)
        for i in range(ROW_CHUNKS)
    ]
    for copy in dout_copies:
        copy.start()
    halo = [
        remote(C_HALO + d - 1, kv.at[core, reach], kv.at[core, reach - d], s + d, h)
        for d in range(1, reach + 1)
    ]
    for d in range(1, reach + 1):
        @pl.when(s + d < seqs)
        def _():
            halo[d - 1].start()

    for b in range(PEERS):
        shift = b * width % 128
        first = b * width - shift
        room = min(width + 128, w_out.shape[1] - first)
        cut = w_out[:, first : first + room][:, shift : shift + width]
        cut = jnp.concatenate([cut, pad], axis=1)
        w_cut[b] = cut

        @pl.when(h == b)
        def _():
            w_own[0] = cut

        @pl.when(across == b)
        def _():
            w_own[1] = cut
    wout_copies = [
        remote(C_WOUT, w_cut.at[sib], w_sib.at[0], s, sib),
        remote(C_WOUT + 1, w_cut.at[diag], w_sib.at[1], s, sib),
    ]
    for copy in wout_copies:
        copy.start()

    passed = [
        remote(C_PASS + d - 1, kv.at[core, reach - d], kv.at[core, reach - d], s, sib)
        for d in range(1, reach + 1)
    ]
    for d in range(1, reach + 1):
        @pl.when(s >= d)
        def _():
            halo[d - 1].wait_recv()
            passed[d - 1].start()

    sib_rows = pl.ds(pl.multiple_of(sib * width, 16), width)
    load_wq.wait()
    load_wk.wait()
    own_rows = pl.ds(pl.multiple_of(h * width, 16), width)
    load_own = [
        pltpu.make_async_copy(w.at[own_rows], weights.at[t, 0], local.at[2 + t])
        for t, w in enumerate((wq_all, wkv_all))
    ]
    for copy in load_own:
        copy.start()
    wsib = [
        remote(C_WSIB + t, w.at[sib_rows], weights.at[t, SIB], s, sib)
        for t, w in enumerate((wq_all, wkv_all))
    ]
    for copy in wsib:
        copy.start()
    for d in range(1, reach + 1):
        @pl.when(s >= d)
        def _():
            passed[d - 1].wait_recv()

    for i in range(ROW_CHUNKS):
        here = pl.ds(i * rows, rows)
        row = lax.broadcasted_iota(jnp.int32, (rows, tokens), 0) + i * rows
        col = lax.broadcasted_iota(jnp.int32, (rows, tokens), 1)
        scores = []
        for j in range(reach + 1):
            score = dot_rows(query[here, :], kv[0, j]) * score_scale
            if j == reach:
                score = jnp.where(col <= row, score, -1e30)
            else:
                score = jnp.where(s >= reach - j, score, -1e30)
                if j == 0:
                    score = jnp.where(col > row, score, -1e30)
            scores.append(score)
        top = scores[0]
        for score in scores[1:]:
            top = jnp.maximum(top, score)
        top = jnp.max(top, axis=1, keepdims=True)
        exps = [jnp.exp(score - top) for score in scores]
        mass = exps[0]
        for e in exps[1:]:
            mass = mass + e
        inverse = 1.0 / jnp.sum(mass, axis=1, keepdims=True)
        for j in range(reach + 1):
            p = exps[j] * inverse
            probs[here, j * tokens : (j + 1) * tokens] = p
            low[here, j * tokens : (j + 1) * tokens] = p.astype(bf16)

    for copy in wout_copies:
        copy.wait_recv()
    for i in range(ROW_CHUNKS):
        here = pl.ds(i * rows, rows)
        heads[here, :] = dot_rows(d_own[here, :], w_own[0])
        partial[here, :] = dot_rows(d_own[here, :], w_sib[0])
    for i in range(ROW_CHUNKS):
        here = pl.ds(i * rows, rows)
        dout_copies[i].wait_recv()
        partial[here, :] += dot_rows(d_far[here, :], w_sib[1])
        heads[here, :] += dot_rows(d_far[here, :], w_own[1])
    part = remote(C_PART, partial, partial_in, s, sib)
    part.start()

    wfar = []
    for n, (slot, peer) in enumerate(((ACROSS, across), (DIAG, diag))):
        src = pl.ds(pl.multiple_of(peer * width + y * half, 16), half)
        dst = pl.ds(pl.multiple_of(y * half, 16), half)
        wfar.append([
            remote(C_WFAR + 2 * t + n, w.at[src], weights.at[t, slot, dst], s, peer)
            for t, w in enumerate((wq_all, wkv_all))
        ])
    for copy in dout_copies:
        copy.wait_send()
    for t in range(2):
        for far in wfar:
            far[t].start()

    def forward(t, n):
        slot = (ACROSS, DIAG)[n]
        mine = pl.ds(pl.multiple_of(y * half, 16), half)
        block = weights.at[t, slot, mine]
        return remote(C_WFWD + 2 * t + n, block, block, pair, h)

    def relay(t):
        for n in range(2):
            wfar[n][t].wait_recv()
            forward(t, n).start()

    part.wait_recv()
    grad_heads = (heads[...] + partial_in[...]).astype(bf16)

    for j in range(reach + 1):
        parts[1, j] = dot_cols(low[:, j * tokens : (j + 1) * tokens], grad_heads).astype(bf16)
    swap = remote(C_SWAP, parts.at[1 - core], parts_in, s, sib)

    @pl.when(core == 0)
    def _():
        swap.start()

    for i in range(ROW_CHUNKS):
        here = pl.ds(i * rows, rows)
        block = grad_heads[i * rows : (i + 1) * rows]
        weighted = []
        products = []
        for j in range(reach + 1):
            p = probs[here, j * tokens : (j + 1) * tokens]
            dp = dot_rows(block, kv[1, j])
            products.append(dp)
            weighted.append(p * dp)
        delta = weighted[0]
        for w in weighted[1:]:
            delta = delta + w
        delta = jnp.sum(delta, axis=1, keepdims=True)
        for j in range(reach + 1):
            p = probs[here, j * tokens : (j + 1) * tokens]
            ds[here, j * tokens : (j + 1) * tokens] = (p * (products[j] - delta)).astype(bf16)
    for j in range(reach + 1):
        parts[0, j] = (
            dot_cols(ds[:, j * tokens : (j + 1) * tokens], query[...]) * score_scale
        ).astype(bf16)

    @pl.when(core == 1)
    def _():
        swap.start()

    grad_query = jnp.zeros((tokens, HEAD), f32)
    for j in range(reach + 1):
        grad_query = grad_query + jnp.dot(
            ds[:, j * tokens : (j + 1) * tokens], kv[0, j], preferred_element_type=f32)
    grads[0, 0] = (grad_query * score_scale).astype(bf16)

    swap.wait_recv()
    back_copies = [
        remote(C_BACK + d - 1, back.at[reach - d], back_in.at[d - 1], s - d, h)
        for d in range(1, reach + 1)
    ]
    for d in range(reach, -1, -1):
        j = reach - d
        kept = jnp.where(core == 0, parts[0, j].astype(f32), parts[1, j].astype(f32))
        both = kept + parts_in[j].astype(f32)
        if d == 0:
            total[...] = both
        else:
            back[j] = both.astype(bf16)

            @pl.when(s >= d)
            def _():
                back_copies[d - 1].start()

    def share(t):
        return [
            remote(C_GRAD + 3 * t + r - 1, grads.at[t, 0], grads.at[t, r], s, peers[r])
            for r in range(1, PEERS)
        ]

    share_query = share(0)
    for copy in share_query:
        copy.start()
    relay(0)
    relay(1)
    for d in range(1, reach + 1):
        @pl.when(s + d < seqs)
        def _():
            back_copies[d - 1].wait_recv()
            total[...] += back_in[d - 1].astype(f32)
    grads[1, 0] = total[...].astype(bf16)
    share_pair = share(1)
    for copy in share_pair:
        copy.start()

    for copy in wsib:
        copy.wait_recv()
    for copy in load_own:
        copy.wait()
    for t in range(2):
        for n in range(2):
            forward(t, n).wait_recv()
    for copy in share_query + share_pair:
        copy.wait_recv()
    left = jnp.concatenate([grads[t, r] for t in range(2) for r in range(PEERS)], axis=1)
    for first in range(0, width, 256):
        size = min(256, width - first)
        right = [weights[t, r, first : first + size] for t in range(2) for r in range(PEERS)]
        acc = dot_rows(left, jnp.concatenate(right, axis=1))
        out[:, first : first + size] = acc.astype(bf16)

    for copy in wout_copies + share_query + share_pair:
        copy.wait_send()
    for copy in (part, wsib[0], wsib[1], swap):
        copy.wait_send()
    for t in range(2):
        for n in range(2):
            wfar[n][t].wait_send()
            forward(t, n).wait_send()
    for d in range(1, reach + 1):
        @pl.when(s + d < seqs)
        def _():
            halo[d - 1].wait_send()

        @pl.when(s >= d)
        def _():
            passed[d - 1].wait_send()
            back_copies[d - 1].wait_send()


def fused(seqs, query, keys, values, d_out, w_out, w_query, w_key, w_value):
    tokens, width = d_out.shape
    wide = -(-width // 128) * 128
    span = (NBR + 1) * tokens
    bf16, f32 = jnp.bfloat16, jnp.float32
    vmem = pl.BlockSpec(memory_space=pltpu.VMEM)
    anywhere = pl.BlockSpec(memory_space=pl.ANY)
    return pl.pallas_call(
        functools.partial(kernel, seqs),
        out_shape=jax.ShapeDtypeStruct((tokens, width), bf16),
        in_specs=[vmem] * 5 + [anywhere] * 3,
        out_specs=vmem,
        scratch_shapes=[
            pltpu.VMEM(w_query.shape, bf16),
            pltpu.VMEM(w_key.shape, bf16),
            pltpu.VMEM((PEERS, HEAD, wide), bf16),
            pltpu.VMEM((2, HEAD, wide), bf16),
            pltpu.VMEM((2, HEAD, wide), bf16),
            pltpu.VMEM((tokens, wide), bf16),
            pltpu.VMEM((tokens, wide), bf16),
            pltpu.VMEM((2, NBR + 1, tokens, HEAD), bf16),
            pltpu.VMEM((tokens, span), f32),
            pltpu.VMEM((tokens, span), bf16),
            pltpu.VMEM((tokens, span), bf16),
            pltpu.VMEM((tokens, HEAD), f32),
            pltpu.VMEM((tokens, HEAD), f32),
            pltpu.VMEM((tokens, HEAD), f32),
            pltpu.VMEM((2, NBR + 1, tokens, HEAD), bf16),
            pltpu.VMEM((NBR + 1, tokens, HEAD), bf16),
            pltpu.VMEM((NBR, tokens, HEAD), bf16),
            pltpu.VMEM((NBR, tokens, HEAD), bf16),
            pltpu.VMEM((2, PEERS, tokens, HEAD), bf16),
            pltpu.VMEM((2, PEERS, width, HEAD), bf16),
            pltpu.VMEM((tokens, HEAD), f32),
            pltpu.SemaphoreType.DMA((C_END,)),
            pltpu.SemaphoreType.DMA((C_END,)),
            pltpu.SemaphoreType.DMA((4,)),
        ],
        compiler_params=pltpu.CompilerParams(
            collective_id=0, has_side_effects=True, vmem_limit_bytes=48 * 1024 * 1024,
        ),
    )(query, keys, values, d_out, w_out, w_query, w_key, w_value)


def solution(mesh):
    in_specs = (
        P("seq", "head"),
        P("seq", "head"),
        P("seq", "head"),
        P("seq", "head"),
        P("head", None),
        P(None, "head"),
        P(None, "head"),
        P(None, "head"),
    )
    out_specs = P("seq", "head")
    seqs, peers = mesh.shape["seq"], mesh.shape["head"]

    def local(query, keys, values, d_out, w_out, w_query, w_key, w_value):
        args = (query, keys, values, d_out, w_out, w_query, w_key, w_value)
        tokens, width = d_out.shape
        fits = peers == PEERS and seqs % 2 == 0 and query.shape[1] == HEAD
        fits = fits and tokens * NBR == WINDOW and width % 32 == 0
        return fused(seqs, *args) if fits else body(*args)

    return jax.shard_map(local, mesh=mesh, in_specs=in_specs, out_specs=out_specs, check_vma=False)
```

```python
import functools

import jax
import jax.numpy as jnp
from jax import lax
from jax.experimental import pallas as pl
from jax.experimental.pallas import tpu as pltpu
from jax.sharding import PartitionSpec as P

WINDOW = 1024
NBR = 4
HEAD = 128


score_scale = 168.0 ** (-0.5)


def from_behind(block, axis, distance):
    devices = range(lax.axis_size(axis))
    route = [(i - distance, i) for i in devices if i - distance in devices]
    return lax.ppermute(block, axis, route)


def dot_rows(left, right):
    return lax.dot_general(
        left, right, (((1,), (1,)), ((), ())), preferred_element_type=jnp.float32
    )


def dot_cols(left, right):
    return lax.dot_general(
        left, right, (((0,), (0,)), ((), ())), preferred_element_type=jnp.float32
    )


def band_backward(query_block, key_band, value_band, grad_block, query_start, key_start):
    length = query_block.shape[0]
    span = key_band.shape[0]
    query_pos = query_start + jnp.arange(length, dtype=jnp.int32)
    key_pos = key_start + jnp.arange(span, dtype=jnp.int32)
    offset = query_pos[:, None] - key_pos[None, :]
    allowed = (key_pos[None, :] >= 0) & (offset >= 0) & (offset < WINDOW)
    scores = dot_rows(query_block, key_band) * score_scale
    masked = jnp.where(allowed, scores, -1e30)
    top = jnp.max(masked, axis=1, keepdims=True)
    weights = jnp.where(allowed, jnp.exp(masked - top), 0.0)
    probs = weights / jnp.sum(weights, axis=1, keepdims=True)
    probs_low = probs.astype(jnp.bfloat16)
    grad_probs = dot_rows(grad_block, value_band)
    delta = jnp.sum(probs * grad_probs, axis=1, keepdims=True)
    grad_scores = (probs * (grad_probs - delta)).astype(jnp.bfloat16)
    grad_query = (
        jnp.dot(grad_scores, key_band, preferred_element_type=jnp.float32) * score_scale
    ).astype(jnp.bfloat16)
    grad_keys = (dot_cols(grad_scores, query_block) * score_scale).astype(jnp.bfloat16)
    grad_values = dot_cols(probs_low, grad_block).astype(jnp.bfloat16)
    return (grad_query, grad_keys, grad_values)


def body(query, keys, values, d_out, w_out, w_query, w_key, w_value):
    length = query.shape[0]
    seq_index = lax.axis_index("seq")
    gathered = lax.all_gather(d_out, "head", axis=1, tiled=True)
    grad_heads = dot_rows(gathered, w_out).astype(jnp.bfloat16)
    reach = NBR
    key_blocks = []
    value_blocks = []
    for distance in range(reach, 0, -1):
        far_keys, far_values = from_behind((keys, values), "seq", distance)
        key_blocks.append(far_keys)
        value_blocks.append(far_values)
    key_band = jnp.concatenate(key_blocks + [keys], axis=0)
    value_band = jnp.concatenate(value_blocks + [values], axis=0)
    query_start = seq_index * length
    grad_query, key_parts, value_parts = band_backward(
        query, key_band, value_band, grad_heads, query_start, query_start - reach * length
    )
    key_total = key_parts[reach * length :].astype(jnp.float32)
    value_total = value_parts[reach * length :].astype(jnp.float32)
    for distance in range(1, reach + 1):
        first = (reach - distance) * length
        outgoing = (key_parts[first : first + length], value_parts[first : first + length])
        back_keys, back_values = from_behind((outgoing[0], outgoing[1]), "seq", -distance)
        key_total = key_total + back_keys.astype(jnp.float32)
        value_total = value_total + back_values.astype(jnp.float32)
    grad_keys = key_total.astype(jnp.bfloat16)
    grad_values = value_total.astype(jnp.bfloat16)
    summed = dot_rows(w_query, grad_query)
    summed = summed + dot_rows(w_key, grad_keys)
    summed = summed + dot_rows(w_value, grad_values)
    reduced = lax.psum_scatter(
        summed.astype(jnp.bfloat16), "head", scatter_dimension=0, tiled=True
    ).astype(jnp.float32)
    return reduced.T.astype(jnp.bfloat16)


PEERS = 4
SIB, ACROSS, DIAG = 1, 2, 3
ROW_CHUNKS = 4
MESH = pl.DeviceIdType.MESH

C_SIB = 0
C_FAR = C_SIB + 3
C_RELAY = C_FAR + 6
C_HALO = C_RELAY + 9
C_PASS = C_HALO + NBR
C_PART = C_PASS + NBR
C_SWAP = C_PART + 3
C_BACK = C_SWAP + 1
C_GRAD = C_BACK + NBR
C_END = C_GRAD + 6


def kernel(
    seqs, query_in, keys_in, values_in, d_out, w_out, w_query, w_key, w_value, out,
    wq_all, wkv_all, wout_all, d_raw, d_own, w_cut, w_heads, query, kv, probs, low, ds,
    own_part, partial, partial_in, parts, parts_in, back, back_in, grads, weights, total,
    send, recv, local,
):
    s = lax.axis_index("seq")
    h = lax.axis_index("head")
    core = lax.rem(h, 2)
    sib = h + 1 - 2 * core
    across = lax.rem(h + 2, 4)
    diag = lax.rem(sib + 2, 4)
    peers = (None, sib, across, diag)
    y = lax.rem(s, 2)
    z = lax.rem(s // 2, 2)
    pair_y = s + 1 - 2 * y
    pair_z = s + 2 - 4 * z
    quarter = 2 * y + z
    quarter_z = 2 * y + 1 - z
    tokens, width = out.shape
    wide = d_own.shape[1]
    reach = NBR
    f32, bf16 = jnp.float32, jnp.bfloat16

    barrier = pltpu.get_barrier_semaphore()
    for r in range(1, PEERS):
        pl.semaphore_signal(barrier, inc=1, device_id=(s, peers[r]), device_id_type=MESH)
    for d in range(1, reach + 1):
        @pl.when(s >= d)
        def _():
            pl.semaphore_signal(barrier, inc=1, device_id=(s - d, h), device_id_type=MESH)

        @pl.when(s + d < seqs)
        def _():
            pl.semaphore_signal(barrier, inc=1, device_id=(s + d, h), device_id_type=MESH)

    def remote(index, src, dst, seq, head):
        return pltpu.make_async_remote_copy(
            src_ref=src, dst_ref=dst, send_sem=send.at[index], recv_sem=recv.at[index],
            device_id=(seq, head), device_id_type=MESH,
        )

    load_wout = pltpu.make_async_copy(w_out, wout_all, local.at[0])
    load_dout = pltpu.make_async_copy(d_out, d_raw, local.at[1])
    load_keys = pltpu.make_async_copy(keys_in, kv.at[0, reach], local.at[2])
    load_values = pltpu.make_async_copy(values_in, kv.at[1, reach], local.at[3])
    load_query = pltpu.make_async_copy(query_in, query, local.at[4])
    load_wq = pltpu.make_async_copy(w_query, wq_all, local.at[5])
    load_wk = pltpu.make_async_copy(w_key, wkv_all, local.at[6])
    load_wv = pltpu.make_async_copy(w_value, wkv_all, local.at[6])
    for copy in (load_wout, load_keys, load_values, load_dout, load_query, load_wq):
        copy.start()

    @pl.when(core == 0)
    def _():
        load_wk.start()

    @pl.when(core == 1)
    def _():
        load_wv.start()

    for d in range(1, reach + 1):
        @pl.when(s < d)
        def _():
            kv[0, reach - d] = jnp.zeros((tokens, HEAD), bf16)
            kv[1, reach - d] = jnp.zeros((tokens, HEAD), bf16)

    pad = jnp.zeros((HEAD, wide - width), bf16)
    load_wout.wait()
    for b in range(PEERS):
        shift = b * width % 128
        first = b * width - shift
        room = min(width + 128, wout_all.shape[1] - first)
        cut = wout_all[:, first : first + room][:, shift : shift + width]
        cut = jnp.concatenate([cut, pad], axis=1)
        w_cut[b] = cut

        @pl.when(h == b)
        def _():
            w_heads[0] = cut

    behind = jnp.minimum(s, reach)
    ahead = jnp.minimum(seqs - 1 - s, reach)
    pl.semaphore_wait(barrier, PEERS - 1 + behind + ahead)

    quarter_rows = (HEAD // 4, width // 4, width // 4)
    slabs = (w_heads, weights.at[0], weights.at[1])
    alls = (None, wq_all, wkv_all)

    def rows_of(t, index):
        size = quarter_rows[t]
        return pl.ds(pl.multiple_of(index * size, 16), size)

    def to_sib(t):
        if t == 0:
            src = w_cut.at[sib]
        else:
            src = alls[t].at[pl.ds(pl.multiple_of(sib * width, 16), width)]
        return remote(C_SIB + t, src, slabs[t].at[SIB], s, sib)

    def to_far(t, slot):
        peer = peers[slot]
        size = quarter_rows[t]
        if t == 0:
            src = w_cut.at[peer, rows_of(t, quarter)]
        else:
            src = alls[t].at[pl.ds(pl.multiple_of(peer * width + quarter * size, 16), size)]
        dst = slabs[t].at[slot, rows_of(t, quarter)]
        return remote(C_FAR + 2 * t + slot - ACROSS, src, dst, s, peer)

    def relay(t, step):
        index, target = ((quarter, pair_z), (quarter, pair_y), (quarter_z, pair_y))[step]
        block = slabs[t].at[pl.ds(ACROSS, 2), rows_of(t, index)]
        return remote(C_RELAY + 3 * t + step, block, block, target, h)

    def relay_first(t):
        for slot in (ACROSS, DIAG):
            to_far(t, slot).wait_recv()
        relay(t, 0).start()
        relay(t, 1).start()

    def relay_second(t):
        relay(t, 0).wait_recv()
        relay(t, 2).start()

    def arrived(t):
        relay(t, 1).wait_recv()
        relay(t, 2).wait_recv()

    for slot in (ACROSS, DIAG):
        to_far(0, slot).start()
    to_sib(0).start()
    load_keys.wait()
    load_values.wait()
    halo = [
        remote(C_HALO + d - 1, kv.at[core, reach], kv.at[core, reach - d], s + d, h)
        for d in range(1, reach + 1)
    ]
    for d in range(1, reach + 1):
        @pl.when(s + d < seqs)
        def _():
            halo[d - 1].start()
    load_dout.wait()
    d_own[...] = jnp.concatenate([d_raw[...], jnp.zeros((tokens, wide - width), bf16)], axis=1)
    relay_first(0)
    load_wq.wait()
    load_wk.wait()
    load_own = []
    for t in (1, 2):
        rows_own = pl.ds(pl.multiple_of(h * width, 16), width)
        load_own.append(
            pltpu.make_async_copy(alls[t].at[rows_own], slabs[t].at[0], local.at[6 + t]))
        for slot in (ACROSS, DIAG):
            to_far(t, slot).start()

    to_sib(0).wait_recv()
    rows = tokens // ROW_CHUNKS
    both_heads = 2 * HEAD
    near = w_heads[0:2].reshape(both_heads, wide)
    for i in range(ROW_CHUNKS):
        here = pl.ds(i * rows, rows)
        result = dot_rows(d_own[here, :], near)
        own_part[here, :] = result[:, :HEAD]
        partial[SIB - 1, here, :] = result[:, HEAD:].astype(bf16)
    part = [
        remote(C_PART + r - 1, partial.at[r - 1], partial_in.at[r - 1], s, peers[r])
        for r in range(1, PEERS)
    ]
    part[SIB - 1].start()
    relay_second(0)
    passed = [
        remote(C_PASS + d - 1, kv.at[core, reach - d], kv.at[core, reach - d], s, sib)
        for d in range(1, reach + 1)
    ]
    for d in range(1, reach + 1):
        @pl.when(s >= d)
        def _():
            halo[d - 1].wait_recv()
            passed[d - 1].start()
    arrived(0)
    far = w_heads[2:4].reshape(both_heads, wide)
    for i in range(ROW_CHUNKS):
        here = pl.ds(i * rows, rows)
        result = dot_rows(d_own[here, :], far)
        partial[ACROSS - 1, here, :] = result[:, :HEAD].astype(bf16)
        partial[DIAG - 1, here, :] = result[:, HEAD:].astype(bf16)
    part[ACROSS - 1].start()
    part[DIAG - 1].start()
    for copy in load_own:
        copy.start()
    for t in (1, 2):
        to_sib(t).start()
    relay_first(1)
    load_query.wait()
    for d in range(1, reach + 1):
        @pl.when(s >= d)
        def _():
            passed[d - 1].wait_recv()

    for i in range(ROW_CHUNKS):
        here = pl.ds(i * rows, rows)
        row = lax.broadcasted_iota(jnp.int32, (rows, tokens), 0) + i * rows
        col = lax.broadcasted_iota(jnp.int32, (rows, tokens), 1)
        scores = []
        for j in range(reach + 1):
            score = dot_rows(query[here, :], kv[0, j]) * score_scale
            if j == reach:
                score = jnp.where(col <= row, score, -1e30)
            else:
                score = jnp.where(s >= reach - j, score, -1e30)
                if j == 0:
                    score = jnp.where(col > row, score, -1e30)
            scores.append(score)
        top = scores[0]
        for score in scores[1:]:
            top = jnp.maximum(top, score)
        top = jnp.max(top, axis=1, keepdims=True)
        exps = [jnp.exp(score - top) for score in scores]
        mass = exps[0]
        for e in exps[1:]:
            mass = mass + e
        inverse = 1.0 / jnp.sum(mass, axis=1, keepdims=True)
        for j in range(reach + 1):
            p = exps[j] * inverse
            probs[here, j * tokens : (j + 1) * tokens] = p
            low[here, j * tokens : (j + 1) * tokens] = p.astype(bf16)

    relay_first(2)
    relay_second(1)
    for copy in part:
        copy.wait_recv()
    grad_heads = own_part[...]
    for r in range(1, PEERS):
        grad_heads = grad_heads + partial_in[r - 1].astype(f32)
    grad_heads = grad_heads.astype(bf16)

    for j in range(reach + 1):
        parts[1, j] = dot_cols(low[:, j * tokens : (j + 1) * tokens], grad_heads).astype(bf16)
    swap = remote(C_SWAP, parts.at[1 - core], parts_in, s, sib)

    @pl.when(core == 0)
    def _():
        swap.start()

    for i in range(ROW_CHUNKS):
        here = pl.ds(i * rows, rows)
        block = grad_heads[i * rows : (i + 1) * rows]
        weighted = []
        products = []
        for j in range(reach + 1):
            p = probs[here, j * tokens : (j + 1) * tokens]
            dp = dot_rows(block, kv[1, j])
            products.append(dp)
            weighted.append(p * dp)
        delta = weighted[0]
        for w in weighted[1:]:
            delta = delta + w
        delta = jnp.sum(delta, axis=1, keepdims=True)
        for j in range(reach + 1):
            p = probs[here, j * tokens : (j + 1) * tokens]
            ds[here, j * tokens : (j + 1) * tokens] = (p * (products[j] - delta)).astype(bf16)
    for j in range(reach + 1):
        parts[0, j] = (
            dot_cols(ds[:, j * tokens : (j + 1) * tokens], query[...]) * score_scale
        ).astype(bf16)

    @pl.when(core == 1)
    def _():
        swap.start()

    grad_query = jnp.zeros((tokens, HEAD), f32)
    for j in range(reach + 1):
        grad_query = grad_query + jnp.dot(
            ds[:, j * tokens : (j + 1) * tokens], kv[0, j], preferred_element_type=f32)
    grads[0, 0] = (grad_query * score_scale).astype(bf16)

    swap.wait_recv()
    back_copies = [
        remote(C_BACK + d - 1, back.at[reach - d], back_in.at[d - 1], s - d, h)
        for d in range(1, reach + 1)
    ]
    for d in range(reach, -1, -1):
        j = reach - d
        kept = jnp.where(core == 0, parts[0, j].astype(f32), parts[1, j].astype(f32))
        both = kept + parts_in[j].astype(f32)
        if d == 0:
            total[...] = both
        else:
            back[j] = both.astype(bf16)

            @pl.when(s >= d)
            def _():
                back_copies[d - 1].start()

    def share(t):
        return [
            remote(C_GRAD + 3 * t + r - 1, grads.at[t, 0], grads.at[t, r], s, peers[r])
            for r in range(1, PEERS)
        ]

    share_query = share(0)
    for copy in share_query:
        copy.start()
    relay_second(2)
    for d in range(1, reach + 1):
        @pl.when(s + d < seqs)
        def _():
            back_copies[d - 1].wait_recv()
            total[...] += back_in[d - 1].astype(f32)
    grads[1, 0] = total[...].astype(bf16)
    share_pair = share(1)
    for copy in share_pair:
        copy.start()

    for copy in load_own:
        copy.wait()
    for t in (1, 2):
        to_sib(t).wait_recv()
        arrived(t)
    for copy in share_query + share_pair:
        copy.wait_recv()
    left = jnp.concatenate([grads[t, r] for t in range(2) for r in range(PEERS)], axis=1)
    for first in range(0, width, 256):
        size = min(256, width - first)
        right = [weights[t, r, first : first + size] for t in range(2) for r in range(PEERS)]
        acc = dot_rows(left, jnp.concatenate(right, axis=1))
        out[:, first : first + size] = acc.astype(bf16)

    for copy in part + share_query + share_pair + [swap]:
        copy.wait_send()
    for t in range(3):
        to_sib(t).wait_send()
        for slot in (ACROSS, DIAG):
            to_far(t, slot).wait_send()
        for step in range(3):
            relay(t, step).wait_send()
    for d in range(1, reach + 1):
        @pl.when(s + d < seqs)
        def _():
            halo[d - 1].wait_send()

        @pl.when(s >= d)
        def _():
            passed[d - 1].wait_send()
            back_copies[d - 1].wait_send()


def fused(seqs, query, keys, values, d_out, w_out, w_query, w_key, w_value):
    tokens, width = d_out.shape
    wide = -(-width // 128) * 128
    span = (NBR + 1) * tokens
    bf16, f32 = jnp.bfloat16, jnp.float32
    vmem = pl.BlockSpec(memory_space=pltpu.VMEM)
    hbm = pl.BlockSpec(memory_space=pltpu.HBM)
    return pl.pallas_call(
        functools.partial(kernel, seqs),
        out_shape=jax.ShapeDtypeStruct((tokens, width), bf16),
        in_specs=[hbm] * 8,
        out_specs=vmem,
        scratch_shapes=[
            pltpu.VMEM(w_query.shape, bf16),
            pltpu.VMEM(w_key.shape, bf16),
            pltpu.VMEM(w_out.shape, bf16),
            pltpu.VMEM((tokens, width), bf16),
            pltpu.VMEM((tokens, wide), bf16),
            pltpu.VMEM((PEERS, HEAD, wide), bf16),
            pltpu.VMEM((PEERS, HEAD, wide), bf16),
            pltpu.VMEM((tokens, HEAD), bf16),
            pltpu.VMEM((2, NBR + 1, tokens, HEAD), bf16),
            pltpu.VMEM((tokens, span), f32),
            pltpu.VMEM((tokens, span), bf16),
            pltpu.VMEM((tokens, span), bf16),
            pltpu.VMEM((tokens, HEAD), f32),
            pltpu.VMEM((PEERS - 1, tokens, HEAD), bf16),
            pltpu.VMEM((PEERS - 1, tokens, HEAD), bf16),
            pltpu.VMEM((2, NBR + 1, tokens, HEAD), bf16),
            pltpu.VMEM((NBR + 1, tokens, HEAD), bf16),
            pltpu.VMEM((NBR, tokens, HEAD), bf16),
            pltpu.VMEM((NBR, tokens, HEAD), bf16),
            pltpu.VMEM((2, PEERS, tokens, HEAD), bf16),
            pltpu.VMEM((2, PEERS, width, HEAD), bf16),
            pltpu.VMEM((tokens, HEAD), f32),
            pltpu.SemaphoreType.DMA((C_END,)),
            pltpu.SemaphoreType.DMA((C_END,)),
            pltpu.SemaphoreType.DMA((9,)),
        ],
        compiler_params=pltpu.CompilerParams(
            collective_id=0, has_side_effects=True, vmem_limit_bytes=48 * 1024 * 1024,
        ),
    )(query, keys, values, d_out, w_out, w_query, w_key, w_value)


def solution(mesh):
    in_specs = (
        P("seq", "head"),
        P("seq", "head"),
        P("seq", "head"),
        P("seq", "head"),
        P("head", None),
        P(None, "head"),
        P(None, "head"),
        P(None, "head"),
    )
    out_specs = P("seq", "head")
    seqs, peers = mesh.shape["seq"], mesh.shape["head"]

    def local(query, keys, values, d_out, w_out, w_query, w_key, w_value):
        args = (query, keys, values, d_out, w_out, w_query, w_key, w_value)
        tokens, width = d_out.shape
        fits = peers == PEERS and seqs % 4 == 0 and query.shape[1] == HEAD
        fits = fits and tokens * NBR == WINDOW and width % 64 == 0
        return fused(seqs, *args) if fits else body(*args)

    return jax.shard_map(local, mesh=mesh, in_specs=in_specs, out_specs=out_specs, check_vma=False)
```

```python
import functools

import jax
import jax.numpy as jnp
from jax import lax
from jax.experimental import pallas as pl
from jax.experimental.pallas import tpu as pltpu
from jax.sharding import PartitionSpec as P

WINDOW = 1024
NBR = 4
HEAD = 128


score_scale = 168.0 ** (-0.5)


def from_behind(block, axis, distance):
    devices = range(lax.axis_size(axis))
    route = [(i - distance, i) for i in devices if i - distance in devices]
    return lax.ppermute(block, axis, route)


def dot_rows(left, right):
    return lax.dot_general(
        left, right, (((1,), (1,)), ((), ())), preferred_element_type=jnp.float32
    )


def dot_cols(left, right):
    return lax.dot_general(
        left, right, (((0,), (0,)), ((), ())), preferred_element_type=jnp.float32
    )


def band_backward(query_block, key_band, value_band, grad_block, query_start, key_start):
    length = query_block.shape[0]
    span = key_band.shape[0]
    query_pos = query_start + jnp.arange(length, dtype=jnp.int32)
    key_pos = key_start + jnp.arange(span, dtype=jnp.int32)
    offset = query_pos[:, None] - key_pos[None, :]
    allowed = (key_pos[None, :] >= 0) & (offset >= 0) & (offset < WINDOW)
    scores = dot_rows(query_block, key_band) * score_scale
    masked = jnp.where(allowed, scores, -1e30)
    top = jnp.max(masked, axis=1, keepdims=True)
    weights = jnp.where(allowed, jnp.exp(masked - top), 0.0)
    probs = weights / jnp.sum(weights, axis=1, keepdims=True)
    probs_low = probs.astype(jnp.bfloat16)
    grad_probs = dot_rows(grad_block, value_band)
    delta = jnp.sum(probs * grad_probs, axis=1, keepdims=True)
    grad_scores = (probs * (grad_probs - delta)).astype(jnp.bfloat16)
    grad_query = (
        jnp.dot(grad_scores, key_band, preferred_element_type=jnp.float32) * score_scale
    ).astype(jnp.bfloat16)
    grad_keys = (dot_cols(grad_scores, query_block) * score_scale).astype(jnp.bfloat16)
    grad_values = dot_cols(probs_low, grad_block).astype(jnp.bfloat16)
    return (grad_query, grad_keys, grad_values)


def body(query, keys, values, d_out, w_out, w_query, w_key, w_value):
    length = query.shape[0]
    seq_index = lax.axis_index("seq")
    gathered = lax.all_gather(d_out, "head", axis=1, tiled=True)
    grad_heads = dot_rows(gathered, w_out).astype(jnp.bfloat16)
    reach = NBR
    key_blocks = []
    value_blocks = []
    for distance in range(reach, 0, -1):
        far_keys, far_values = from_behind((keys, values), "seq", distance)
        key_blocks.append(far_keys)
        value_blocks.append(far_values)
    key_band = jnp.concatenate(key_blocks + [keys], axis=0)
    value_band = jnp.concatenate(value_blocks + [values], axis=0)
    query_start = seq_index * length
    grad_query, key_parts, value_parts = band_backward(
        query, key_band, value_band, grad_heads, query_start, query_start - reach * length
    )
    key_total = key_parts[reach * length :].astype(jnp.float32)
    value_total = value_parts[reach * length :].astype(jnp.float32)
    for distance in range(1, reach + 1):
        first = (reach - distance) * length
        outgoing = (key_parts[first : first + length], value_parts[first : first + length])
        back_keys, back_values = from_behind((outgoing[0], outgoing[1]), "seq", -distance)
        key_total = key_total + back_keys.astype(jnp.float32)
        value_total = value_total + back_values.astype(jnp.float32)
    grad_keys = key_total.astype(jnp.bfloat16)
    grad_values = value_total.astype(jnp.bfloat16)
    summed = dot_rows(w_query, grad_query)
    summed = summed + dot_rows(w_key, grad_keys)
    summed = summed + dot_rows(w_value, grad_values)
    reduced = lax.psum_scatter(
        summed.astype(jnp.bfloat16), "head", scatter_dimension=0, tiled=True
    ).astype(jnp.float32)
    return reduced.T.astype(jnp.bfloat16)


PEERS = 4
SIB, ACROSS, DIAG = 1, 2, 3
ROW_CHUNKS = 4
MESH = pl.DeviceIdType.MESH

C_SIB = 0
C_FAR = C_SIB + 3
C_RELAY = C_FAR + 8
C_HALO = C_RELAY + 24
C_PASS = C_HALO + NBR
C_PART = C_PASS + NBR
C_SWAP = C_PART + 3
C_BACK = C_SWAP + 1
C_GRAD = C_BACK + NBR
C_END = C_GRAD + 6


def kernel(
    seqs, query_in, keys_in, values_in, d_out, w_out, w_query, w_key, w_value, out,
    wq_all, wkv_all, wout_all, d_own, w_cut, w_heads, query, kv, probs, low, ds,
    own_part, partial, partial_in, parts, parts_in, back, back_in, grads, weights, total, acc,
    send, recv, local,
):
    s = lax.axis_index("seq")
    h = lax.axis_index("head")
    core = lax.rem(h, 2)
    sib = h + 1 - 2 * core
    across = lax.rem(h + 2, 4)
    diag = lax.rem(sib + 2, 4)
    peers = (None, sib, across, diag)
    y = lax.rem(s, 2)
    z = lax.rem(s // 2, 2)
    pair_y = s + 1 - 2 * y
    pair_z = s + 2 - 4 * z
    quarter = 2 * y + z
    quarter_z = 2 * y + 1 - z
    quarter_y = 2 - 2 * y + z
    width, tokens = out.shape
    wide = d_own.shape[0]
    reach = NBR
    f32, bf16 = jnp.float32, jnp.bfloat16

    barrier = pltpu.get_barrier_semaphore()
    for r in range(1, PEERS):
        pl.semaphore_signal(barrier, inc=1, device_id=(s, peers[r]), device_id_type=MESH)
    for d in range(1, reach + 1):
        @pl.when(s >= d)
        def _():
            pl.semaphore_signal(barrier, inc=1, device_id=(s - d, h), device_id_type=MESH)

        @pl.when(s + d < seqs)
        def _():
            pl.semaphore_signal(barrier, inc=1, device_id=(s + d, h), device_id_type=MESH)

    def remote(index, src, dst, seq, head):
        return pltpu.make_async_remote_copy(
            src_ref=src, dst_ref=dst, send_sem=send.at[index], recv_sem=recv.at[index],
            device_id=(seq, head), device_id_type=MESH,
        )

    load_wout = pltpu.make_async_copy(w_out, wout_all, local.at[0])
    load_dout = pltpu.make_async_copy(d_out, d_own.at[pl.ds(0, width)], local.at[1])
    load_keys = pltpu.make_async_copy(keys_in, kv.at[0, reach], local.at[2])
    load_values = pltpu.make_async_copy(values_in, kv.at[1, reach], local.at[3])
    load_query = pltpu.make_async_copy(query_in, query, local.at[4])
    load_wq = pltpu.make_async_copy(w_query, wq_all, local.at[5])
    load_wk = pltpu.make_async_copy(w_key, wkv_all, local.at[6])
    load_wv = pltpu.make_async_copy(w_value, wkv_all, local.at[6])
    for copy in (load_wout, load_keys, load_values, load_dout, load_query, load_wq):
        copy.start()

    @pl.when(core == 0)
    def _():
        load_wk.start()

    @pl.when(core == 1)
    def _():
        load_wv.start()

    for d in range(1, reach + 1):
        @pl.when(s < d)
        def _():
            kv[0, reach - d] = jnp.zeros((tokens, HEAD), bf16)
            kv[1, reach - d] = jnp.zeros((tokens, HEAD), bf16)

    d_own[width:wide] = jnp.zeros((wide - width, tokens), bf16)

    pad = jnp.zeros((HEAD, wide - width), bf16)
    load_wout.wait()
    for b in range(PEERS):
        shift = b * width % 128
        first = b * width - shift
        room = min(width + 128, wout_all.shape[1] - first)
        cut = wout_all[:, first : first + room][:, shift : shift + width]
        cut = jnp.concatenate([cut, pad], axis=1)
        w_cut[b] = cut

        @pl.when(h == b)
        def _():
            w_heads[0] = cut

    behind = jnp.minimum(s, reach)
    ahead = jnp.minimum(seqs - 1 - s, reach)
    pl.semaphore_wait(barrier, PEERS - 1 + behind + ahead)

    piece = (HEAD // 8, HEAD // 8, width // 4, width // 4)
    slab_of = (0, 0, 1, 2)
    slabs = (w_heads, weights.at[0], weights.at[1])
    alls = (None, wq_all, wkv_all)

    def start_of(i, index):
        return index * 2 * piece[i] + i * piece[i] if i < 2 else index * piece[i]

    def rows_of(i, index):
        return pl.ds(pl.multiple_of(start_of(i, index), 16), piece[i])

    def to_sib(t):
        if t == 0:
            src = w_cut.at[sib]
        else:
            src = alls[t].at[pl.ds(pl.multiple_of(sib * width, 16), width)]
        return remote(C_SIB + t, src, slabs[t].at[SIB], s, sib)

    def to_far(i, slot):
        peer = peers[slot]
        t = slab_of[i]
        if t == 0:
            src = w_cut.at[peer, rows_of(i, quarter)]
        else:
            first = peer * width + start_of(i, quarter)
            src = alls[t].at[pl.ds(pl.multiple_of(first, 16), piece[i])]
        dst = slabs[t].at[slot, rows_of(i, quarter)]
        return remote(C_FAR + 2 * i + slot - ACROSS, src, dst, s, peer)

    def relay(i, slot, step):
        if step < 2:
            index, target = quarter, (pair_z, pair_y)[step]
        elif slab_of[i] == 0 and slot == DIAG:
            index, target = quarter_y, pair_z
        else:
            index, target = quarter_z, pair_y
        block = slabs[slab_of[i]].at[slot, rows_of(i, index)]
        number = 6 * i + 3 * (slot - ACROSS) + step
        return remote(C_RELAY + number, block, block, target, h)

    def relay_first(i):
        for slot in (ACROSS, DIAG):
            to_far(i, slot).wait_recv()
            relay(i, slot, 0).start()
            relay(i, slot, 1).start()

    def relay_second(i):
        for slot in (ACROSS, DIAG):
            over_y = slab_of[i] == 0 and slot == DIAG
            relay(i, slot, 1 if over_y else 0).wait_recv()
            relay(i, slot, 2).start()

    def arrived(i):
        for slot in (ACROSS, DIAG):
            over_y = slab_of[i] == 0 and slot == DIAG
            relay(i, slot, 0 if over_y else 1).wait_recv()
            relay(i, slot, 2).wait_recv()

    for i in (0, 1):
        for slot in (ACROSS, DIAG):
            to_far(i, slot).start()
    to_sib(0).start()
    load_keys.wait()
    load_values.wait()
    halo = [
        remote(C_HALO + d - 1, kv.at[core, reach], kv.at[core, reach - d], s + d, h)
        for d in range(1, reach + 1)
    ]
    passed = [
        remote(C_PASS + d - 1, kv.at[core, reach - d], kv.at[core, reach - d], s, sib)
        for d in range(1, reach + 1)
    ]

    def send_halo(which):
        for d in range(1, reach + 1):
            @pl.when((core == which) & (s + d < seqs))
            def _():
                halo[d - 1].start()

    def pass_halo(which):
        for d in range(1, reach + 1):
            @pl.when((core == which) & (s >= d))
            def _():
                halo[d - 1].wait_recv()
                passed[d - 1].start()

    def get_halo(which):
        for d in range(1, reach + 1):
            @pl.when((core != which) & (s >= d))
            def _():
                passed[d - 1].wait_recv()

    send_halo(0)
    load_dout.wait()
    load_wq.wait()
    load_wk.wait()
    load_own = []
    for t in (1, 2):
        rows_own = pl.ds(pl.multiple_of(h * width, 16), width)
        load_own.append(
            pltpu.make_async_copy(alls[t].at[rows_own], slabs[t].at[0], local.at[6 + t]))
    relay_first(0)
    relay_first(1)
    for slot in (ACROSS, DIAG):
        to_far(2, slot).start()

    to_sib(0).wait_recv()
    rows = tokens // ROW_CHUNKS
    both_heads = 2 * HEAD
    d_all = d_own[...]
    near = w_heads[0:2].reshape(both_heads, wide)
    result = jnp.dot(near, d_all, preferred_element_type=f32).T
    own_part[...] = result[:, :HEAD]
    partial[SIB - 1] = result[:, HEAD:].astype(bf16)
    part = [
        remote(C_PART + r - 1, partial.at[r - 1], partial_in.at[r - 1], s, peers[r])
        for r in range(1, PEERS)
    ]
    part[SIB - 1].start()
    relay_second(0)
    relay_second(1)
    send_halo(1)
    pass_halo(0)
    arrived(0)
    arrived(1)
    far = w_heads[2:4].reshape(both_heads, wide)
    result = jnp.dot(far, d_all, preferred_element_type=f32).T.astype(bf16)
    partial[ACROSS - 1] = result[:, :HEAD]
    partial[DIAG - 1] = result[:, HEAD:]
    part[ACROSS - 1].start()
    part[DIAG - 1].start()
    for copy in load_own:
        copy.start()
    for t in (1, 2):
        to_sib(t).start()
    relay_first(2)
    load_query.wait()
    get_halo(0)

    for i in range(ROW_CHUNKS):
        here = pl.ds(i * rows, rows)
        row = lax.broadcasted_iota(jnp.int32, (rows, tokens), 0) + i * rows
        col = lax.broadcasted_iota(jnp.int32, (rows, tokens), 1)
        scores = []
        for j in range(reach + 1):
            score = dot_rows(query[here, :], kv[0, j]) * score_scale
            if j == reach:
                score = jnp.where(col <= row, score, -1e30)
            else:
                score = jnp.where(s >= reach - j, score, -1e30)
                if j == 0:
                    score = jnp.where(col > row, score, -1e30)
            scores.append(score)
        top = scores[0]
        for score in scores[1:]:
            top = jnp.maximum(top, score)
        top = jnp.max(top, axis=1, keepdims=True)
        exps = [jnp.exp(score - top) for score in scores]
        mass = exps[0]
        for e in exps[1:]:
            mass = mass + e
        inverse = 1.0 / jnp.sum(mass, axis=1, keepdims=True)
        for j in range(reach + 1):
            p = exps[j] * inverse
            probs[here, j * tokens : (j + 1) * tokens] = p
            low[here, j * tokens : (j + 1) * tokens] = p.astype(bf16)

    pass_halo(1)
    relay_second(2)
    for copy in part:
        copy.wait_recv()
    for slot in (ACROSS, DIAG):
        to_far(3, slot).start()
    grad_heads = own_part[...]
    for r in range(1, PEERS):
        grad_heads = grad_heads + partial_in[r - 1].astype(f32)
    grad_heads = grad_heads.astype(bf16)

    for j in range(reach + 1):
        parts[1, j] = dot_cols(low[:, j * tokens : (j + 1) * tokens], grad_heads).astype(bf16)
    swap = remote(C_SWAP, parts.at[1 - core], parts_in, s, sib)

    @pl.when(core == 0)
    def _():
        swap.start()

    back_copies = [
        remote(C_BACK + d - 1, back.at[reach - d], back_in.at[d - 1], s - d, h)
        for d in range(1, reach + 1)
    ]

    def send_back(which):
        @pl.when(core == which)
        def _():
            swap.wait_recv()
            for d in range(reach, -1, -1):
                j = reach - d
                both = parts[which, j].astype(f32) + parts_in[j].astype(f32)
                if d == 0:
                    total[...] = both
                else:
                    back[j] = both.astype(bf16)

                    @pl.when(s >= d)
                    def _():
                        back_copies[d - 1].start()

    get_halo(1)
    for i in range(ROW_CHUNKS):
        if i == ROW_CHUNKS // 2:
            send_back(1)
        here = pl.ds(i * rows, rows)
        block = grad_heads[i * rows : (i + 1) * rows]
        weighted = []
        products = []
        for j in range(reach + 1):
            p = probs[here, j * tokens : (j + 1) * tokens]
            dp = dot_rows(block, kv[1, j])
            products.append(dp)
            weighted.append(p * dp)
        delta = weighted[0]
        for w in weighted[1:]:
            delta = delta + w
        delta = jnp.sum(delta, axis=1, keepdims=True)
        for j in range(reach + 1):
            p = probs[here, j * tokens : (j + 1) * tokens]
            ds[here, j * tokens : (j + 1) * tokens] = (p * (products[j] - delta)).astype(bf16)
    for j in range(reach + 1):
        parts[0, j] = (
            dot_cols(ds[:, j * tokens : (j + 1) * tokens], query[...]) * score_scale
        ).astype(bf16)

    @pl.when(core == 1)
    def _():
        swap.start()

    grad_query = jnp.zeros((tokens, HEAD), f32)
    for j in range(reach + 1):
        grad_query = grad_query + jnp.dot(
            ds[:, j * tokens : (j + 1) * tokens], kv[0, j], preferred_element_type=f32)
    grads[0, 0] = (grad_query * score_scale).astype(bf16)

    send_back(0)

    def share(t):
        return [
            remote(C_GRAD + 3 * t + r - 1, grads.at[t, 0], grads.at[t, r], s, peers[r])
            for r in range(1, PEERS)
        ]

    share_query = share(0)
    for copy in share_query:
        copy.start()
    relay_first(3)

    for copy in share_query:
        copy.wait_recv()
    load_own[0].wait()
    to_sib(1).wait_recv()
    arrived(2)
    chunk = width // 7

    def product(t, first):
        right = jnp.concatenate([grads[t, r] for r in range(PEERS)], axis=1)
        left = jnp.concatenate(
            [weights[t, r, first : first + chunk] for r in range(PEERS)], axis=1)
        return dot_rows(left, right)

    for first in range(0, width, chunk):
        acc[first : first + chunk] = product(0, first)
    relay_second(3)
    for d in range(1, reach + 1):
        @pl.when(s + d < seqs)
        def _():
            back_copies[d - 1].wait_recv()
            total[...] += back_in[d - 1].astype(f32)
    grads[1, 0] = total[...].astype(bf16)
    share_pair = share(1)
    for copy in share_pair:
        copy.start()

    load_own[1].wait()
    to_sib(2).wait_recv()
    arrived(3)
    for copy in share_pair:
        copy.wait_recv()
    for first in range(0, width, chunk):
        here = slice(first, first + chunk)
        out[here] = (acc[here] + product(1, first)).astype(bf16)

    for copy in part + share_query + share_pair + [swap]:
        copy.wait_send()
    for t in range(3):
        to_sib(t).wait_send()
    for i in range(4):
        for slot in (ACROSS, DIAG):
            to_far(i, slot).wait_send()
            for step in range(3):
                relay(i, slot, step).wait_send()
    for d in range(1, reach + 1):
        @pl.when(s + d < seqs)
        def _():
            halo[d - 1].wait_send()

        @pl.when(s >= d)
        def _():
            passed[d - 1].wait_send()
            back_copies[d - 1].wait_send()


def fused(seqs, query, keys, values, d_out, w_out, w_query, w_key, w_value):
    tokens, width = d_out.shape
    wide = -(-width // 128) * 128
    span = (NBR + 1) * tokens
    bf16, f32 = jnp.bfloat16, jnp.float32
    vmem = pl.BlockSpec(memory_space=pltpu.VMEM)
    hbm = pl.BlockSpec(memory_space=pltpu.HBM)
    return pl.pallas_call(
        functools.partial(kernel, seqs),
        out_shape=jax.ShapeDtypeStruct((width, tokens), bf16),
        in_specs=[hbm] * 8,
        out_specs=vmem,
        scratch_shapes=[
            pltpu.VMEM(w_query.shape, bf16),
            pltpu.VMEM(w_key.shape, bf16),
            pltpu.VMEM(w_out.shape, bf16),
            pltpu.VMEM((wide, tokens), bf16),
            pltpu.VMEM((PEERS, HEAD, wide), bf16),
            pltpu.VMEM((PEERS, HEAD, wide), bf16),
            pltpu.VMEM((tokens, HEAD), bf16),
            pltpu.VMEM((2, NBR + 1, tokens, HEAD), bf16),
            pltpu.VMEM((tokens, span), f32),
            pltpu.VMEM((tokens, span), bf16),
            pltpu.VMEM((tokens, span), bf16),
            pltpu.VMEM((tokens, HEAD), f32),
            pltpu.VMEM((PEERS - 1, tokens, HEAD), bf16),
            pltpu.VMEM((PEERS - 1, tokens, HEAD), bf16),
            pltpu.VMEM((2, NBR + 1, tokens, HEAD), bf16),
            pltpu.VMEM((NBR + 1, tokens, HEAD), bf16),
            pltpu.VMEM((NBR, tokens, HEAD), bf16),
            pltpu.VMEM((NBR, tokens, HEAD), bf16),
            pltpu.VMEM((2, PEERS, tokens, HEAD), bf16),
            pltpu.VMEM((2, PEERS, width, HEAD), bf16),
            pltpu.VMEM((tokens, HEAD), f32),
            pltpu.VMEM((width, tokens), f32),
            pltpu.SemaphoreType.DMA((C_END,)),
            pltpu.SemaphoreType.DMA((C_END,)),
            pltpu.SemaphoreType.DMA((9,)),
        ],
        compiler_params=pltpu.CompilerParams(
            collective_id=0, has_side_effects=True, vmem_limit_bytes=63 * 1024 * 1024,
        ),
    )(query, keys, values, d_out.T, w_out, w_query, w_key, w_value).T


def solution(mesh):
    in_specs = (
        P("seq", "head"),
        P("seq", "head"),
        P("seq", "head"),
        P("seq", "head"),
        P("head", None),
        P(None, "head"),
        P(None, "head"),
        P(None, "head"),
    )
    out_specs = P("seq", "head")
    seqs, peers = mesh.shape["seq"], mesh.shape["head"]

    def local(query, keys, values, d_out, w_out, w_query, w_key, w_value):
        args = (query, keys, values, d_out, w_out, w_query, w_key, w_value)
        tokens, width = d_out.shape
        fits = peers == PEERS and seqs % 4 == 0 and query.shape[1] == HEAD
        fits = fits and tokens * NBR == WINDOW and width % (64 * 7) == 0
        return fused(seqs, *args) if fits else body(*args)

    return jax.shard_map(local, mesh=mesh, in_specs=in_specs, out_specs=out_specs, check_vma=False)
```

```python
import functools

import jax
import jax.numpy as jnp
from jax import lax
from jax.experimental import pallas as pl
from jax.experimental.pallas import tpu as pltpu
from jax.sharding import PartitionSpec as P

WINDOW = 1024
NBR = 4
HEAD = 128


score_scale = 168.0 ** (-0.5)


def from_behind(block, axis, distance):
    devices = range(lax.axis_size(axis))
    route = [(i - distance, i) for i in devices if i - distance in devices]
    return lax.ppermute(block, axis, route)


def dot_rows(left, right):
    return lax.dot_general(
        left, right, (((1,), (1,)), ((), ())), preferred_element_type=jnp.float32
    )


def dot_cols(left, right):
    return lax.dot_general(
        left, right, (((0,), (0,)), ((), ())), preferred_element_type=jnp.float32
    )


def band_backward(query_block, key_band, value_band, grad_block, query_start, key_start):
    length = query_block.shape[0]
    span = key_band.shape[0]
    query_pos = query_start + jnp.arange(length, dtype=jnp.int32)
    key_pos = key_start + jnp.arange(span, dtype=jnp.int32)
    offset = query_pos[:, None] - key_pos[None, :]
    allowed = (key_pos[None, :] >= 0) & (offset >= 0) & (offset < WINDOW)
    scores = dot_rows(query_block, key_band) * score_scale
    masked = jnp.where(allowed, scores, -1e30)
    top = jnp.max(masked, axis=1, keepdims=True)
    weights = jnp.where(allowed, jnp.exp(masked - top), 0.0)
    probs = weights / jnp.sum(weights, axis=1, keepdims=True)
    probs_low = probs.astype(jnp.bfloat16)
    grad_probs = dot_rows(grad_block, value_band)
    delta = jnp.sum(probs * grad_probs, axis=1, keepdims=True)
    grad_scores = (probs * (grad_probs - delta)).astype(jnp.bfloat16)
    grad_query = (
        jnp.dot(grad_scores, key_band, preferred_element_type=jnp.float32) * score_scale
    ).astype(jnp.bfloat16)
    grad_keys = (dot_cols(grad_scores, query_block) * score_scale).astype(jnp.bfloat16)
    grad_values = dot_cols(probs_low, grad_block).astype(jnp.bfloat16)
    return (grad_query, grad_keys, grad_values)


def body(query, keys, values, d_out, w_out, w_query, w_key, w_value):
    length = query.shape[0]
    seq_index = lax.axis_index("seq")
    gathered = lax.all_gather(d_out, "head", axis=1, tiled=True)
    grad_heads = dot_rows(gathered, w_out).astype(jnp.bfloat16)
    reach = NBR
    key_blocks = []
    value_blocks = []
    for distance in range(reach, 0, -1):
        far_keys, far_values = from_behind((keys, values), "seq", distance)
        key_blocks.append(far_keys)
        value_blocks.append(far_values)
    key_band = jnp.concatenate(key_blocks + [keys], axis=0)
    value_band = jnp.concatenate(value_blocks + [values], axis=0)
    query_start = seq_index * length
    grad_query, key_parts, value_parts = band_backward(
        query, key_band, value_band, grad_heads, query_start, query_start - reach * length
    )
    key_total = key_parts[reach * length :].astype(jnp.float32)
    value_total = value_parts[reach * length :].astype(jnp.float32)
    for distance in range(1, reach + 1):
        first = (reach - distance) * length
        outgoing = (key_parts[first : first + length], value_parts[first : first + length])
        back_keys, back_values = from_behind((outgoing[0], outgoing[1]), "seq", -distance)
        key_total = key_total + back_keys.astype(jnp.float32)
        value_total = value_total + back_values.astype(jnp.float32)
    grad_keys = key_total.astype(jnp.bfloat16)
    grad_values = value_total.astype(jnp.bfloat16)
    summed = dot_rows(w_query, grad_query)
    summed = summed + dot_rows(w_key, grad_keys)
    summed = summed + dot_rows(w_value, grad_values)
    reduced = lax.psum_scatter(
        summed.astype(jnp.bfloat16), "head", scatter_dimension=0, tiled=True
    ).astype(jnp.float32)
    return reduced.T.astype(jnp.bfloat16)


PEERS = 4
SIB, ACROSS, DIAG = 1, 2, 3
ROW_CHUNKS = 4
MESH = pl.DeviceIdType.MESH

C_SIB = 0
C_FAR = C_SIB + 3
C_RELAY = C_FAR + 10
C_HALO = C_RELAY + 30
C_PASS = C_HALO + NBR
C_PART = C_PASS + NBR
C_SWAP = C_PART + 3
C_BACK = C_SWAP + 1
C_GRAD = C_BACK + NBR
C_END = C_GRAD + 6


def kernel(
    seqs, query_in, keys_in, values_in, d_out, w_out, w_query, w_key, w_value, out,
    wq_all, wkv_all, wout_all, d_own, w_cut, w_heads, query, kv, probs, low, ds,
    own_part, partial, partial_in, parts, parts_in, back, back_in, grads, weights, total, acc,
    send, recv, local,
):
    s = lax.axis_index("seq")
    h = lax.axis_index("head")
    core = lax.rem(h, 2)
    sib = h + 1 - 2 * core
    across = lax.rem(h + 2, 4)
    diag = lax.rem(sib + 2, 4)
    peers = (None, sib, across, diag)
    y = lax.rem(s, 2)
    z = lax.rem(s // 2, 2)
    pair_y = s + 1 - 2 * y
    pair_z = s + 2 - 4 * z
    quarter = 2 * y + z
    quarter_z = 2 * y + 1 - z
    quarter_y = 2 - 2 * y + z
    width, tokens = out.shape
    wide = d_own.shape[0]
    reach = NBR
    f32, bf16 = jnp.float32, jnp.bfloat16

    barrier = pltpu.get_barrier_semaphore()
    for r in range(1, PEERS):
        pl.semaphore_signal(barrier, inc=1, device_id=(s, peers[r]), device_id_type=MESH)
    for d in range(1, reach + 1):
        @pl.when(s >= d)
        def _():
            pl.semaphore_signal(barrier, inc=1, device_id=(s - d, h), device_id_type=MESH)

        @pl.when(s + d < seqs)
        def _():
            pl.semaphore_signal(barrier, inc=1, device_id=(s + d, h), device_id_type=MESH)

    def remote(index, src, dst, seq, head):
        return pltpu.make_async_remote_copy(
            src_ref=src, dst_ref=dst, send_sem=send.at[index], recv_sem=recv.at[index],
            device_id=(seq, head), device_id_type=MESH,
        )

    load_wout = pltpu.make_async_copy(w_out, wout_all, local.at[0])
    load_dout = pltpu.make_async_copy(d_out, d_own.at[pl.ds(0, width)], local.at[1])
    load_keys = pltpu.make_async_copy(keys_in, kv.at[0, reach], local.at[2])
    load_values = pltpu.make_async_copy(values_in, kv.at[1, reach], local.at[3])
    load_query = pltpu.make_async_copy(query_in, query, local.at[4])
    load_wq = pltpu.make_async_copy(w_query, wq_all, local.at[5])
    load_wk = pltpu.make_async_copy(w_key, wkv_all, local.at[6])
    load_wv = pltpu.make_async_copy(w_value, wkv_all, local.at[6])
    for copy in (load_wout, load_keys, load_values, load_dout, load_query):
        copy.start()

    for d in range(1, reach + 1):
        @pl.when(s < d)
        def _():
            kv[0, reach - d] = jnp.zeros((tokens, HEAD), bf16)
            kv[1, reach - d] = jnp.zeros((tokens, HEAD), bf16)

    d_own[width:wide] = jnp.zeros((wide - width, tokens), bf16)

    pad = jnp.zeros((HEAD, wide - width), bf16)
    load_wout.wait()
    load_wq.start()

    @pl.when(core == 0)
    def _():
        load_wk.start()

    @pl.when(core == 1)
    def _():
        load_wv.start()

    for b in range(PEERS):
        shift = b * width % 128
        first = b * width - shift
        room = min(width + 128, wout_all.shape[1] - first)
        cut = wout_all[:, first : first + room][:, shift : shift + width]
        cut = jnp.concatenate([cut, pad], axis=1)
        w_cut[b] = cut

        @pl.when(h == b)
        def _():
            w_heads[0] = cut

    behind = jnp.minimum(s, reach)
    ahead = jnp.minimum(seqs - 1 - s, reach)
    pl.semaphore_wait(barrier, PEERS - 1 + behind + ahead)

    piece = (HEAD // 8, HEAD // 8, width // 4, width // 4, width // 4)
    slab_of = (0, 0, 1, 2, 2)
    slabs = (w_heads, weights.at[0], weights.at[1])
    alls = (None, wq_all, wkv_all)

    def start_of(i, index):
        if slab_of[i] == 0:
            return (index * 2 + i) * piece[i]
        if slab_of[i] == 1:
            return index * piece[i]
        return (2 * y + i - 3) * piece[i]

    def rows_of(i, index):
        return pl.ds(pl.multiple_of(start_of(i, index), 16), piece[i])

    def to_sib(t):
        if t == 0:
            src = w_cut.at[sib]
        else:
            src = alls[t].at[pl.ds(pl.multiple_of(sib * width, 16), width)]
        return remote(C_SIB + t, src, slabs[t].at[SIB], s, sib)

    def to_far(i, slot):
        peer = peers[slot]
        t = slab_of[i]
        if t == 0:
            src = w_cut.at[peer, rows_of(i, quarter)]
        else:
            first = peer * width + start_of(i, quarter)
            src = alls[t].at[pl.ds(pl.multiple_of(first, 16), piece[i])]
        dst = slabs[t].at[slot, rows_of(i, quarter)]
        return remote(C_FAR + 2 * i + slot - ACROSS, src, dst, s, peer)

    def relay(i, slot, step):
        if step < 2:
            index, target = quarter, (pair_z, pair_y)[step]
        elif slab_of[i] == 0 and slot == DIAG:
            index, target = quarter_y, pair_z
        else:
            index, target = quarter_z, pair_y
        block = slabs[slab_of[i]].at[slot, rows_of(i, index)]
        number = 6 * i + 3 * (slot - ACROSS) + step
        return remote(C_RELAY + number, block, block, target, h)

    def steps_of(i):
        return (1,) if slab_of[i] == 2 else (0, 1, 2)

    def relay_first(i):
        for slot in (ACROSS, DIAG):
            to_far(i, slot).wait_recv()
            for step in steps_of(i)[:2]:
                relay(i, slot, step).start()

    def relay_second(i):
        for slot in (ACROSS, DIAG):
            over_y = slab_of[i] == 0 and slot == DIAG
            relay(i, slot, 1 if over_y else 0).wait_recv()
            relay(i, slot, 2).start()

    def arrived(i):
        for slot in (ACROSS, DIAG):
            over_y = slab_of[i] == 0 and slot == DIAG
            relay(i, slot, 0 if over_y else 1).wait_recv()
            if slab_of[i] < 2:
                relay(i, slot, 2).wait_recv()

    for i in (0, 1):
        for slot in (ACROSS, DIAG):
            to_far(i, slot).start()
    to_sib(0).start()
    load_keys.wait()
    load_values.wait()
    halo = [
        remote(C_HALO + d - 1, kv.at[core, reach], kv.at[core, reach - d], s + d, h)
        for d in range(1, reach + 1)
    ]
    passed = [
        remote(C_PASS + d - 1, kv.at[core, reach - d], kv.at[core, reach - d], s, sib)
        for d in range(1, reach + 1)
    ]

    def send_halo(which):
        for d in range(1, reach + 1):
            @pl.when((core == which) & (s + d < seqs))
            def _():
                halo[d - 1].start()

    def pass_halo(which):
        for d in range(1, reach + 1):
            @pl.when((core == which) & (s >= d))
            def _():
                halo[d - 1].wait_recv()
                passed[d - 1].start()

    def get_halo(which):
        for d in range(1, reach + 1):
            @pl.when((core != which) & (s >= d))
            def _():
                passed[d - 1].wait_recv()

    send_halo(0)
    load_dout.wait()
    load_wq.wait()
    load_wk.wait()
    load_own = []
    for t in (1, 2):
        rows_own = pl.ds(pl.multiple_of(h * width, 16), width)
        load_own.append(
            pltpu.make_async_copy(alls[t].at[rows_own], slabs[t].at[0], local.at[6 + t]))
    relay_first(0)
    relay_first(1)
    for slot in (ACROSS, DIAG):
        to_far(2, slot).start()

    to_sib(0).wait_recv()
    rows = tokens // ROW_CHUNKS
    both_heads = 2 * HEAD
    d_all = d_own[...]
    near = w_heads[0:2].reshape(both_heads, wide)
    result = jnp.dot(near, d_all, preferred_element_type=f32).T
    own_part[...] = result[:, :HEAD]
    partial[SIB - 1] = result[:, HEAD:].astype(bf16)
    part = [
        remote(C_PART + r - 1, partial.at[r - 1], partial_in.at[r - 1], s, peers[r])
        for r in range(1, PEERS)
    ]
    part[SIB - 1].start()
    relay_second(0)
    relay_second(1)
    send_halo(1)
    pass_halo(0)
    arrived(0)
    arrived(1)
    far = w_heads[2:4].reshape(both_heads, wide)
    result = jnp.dot(far, d_all, preferred_element_type=f32).T.astype(bf16)
    partial[ACROSS - 1] = result[:, :HEAD]
    partial[DIAG - 1] = result[:, HEAD:]
    part[ACROSS - 1].start()
    part[DIAG - 1].start()
    for copy in load_own:
        copy.start()
    for t in (1, 2):
        to_sib(t).start()
    relay_first(2)
    load_query.wait()
    get_halo(0)

    for i in range(ROW_CHUNKS):
        here = pl.ds(i * rows, rows)
        row = lax.broadcasted_iota(jnp.int32, (rows, tokens), 0) + i * rows
        col = lax.broadcasted_iota(jnp.int32, (rows, tokens), 1)
        scores = []
        for j in range(reach + 1):
            score = dot_rows(query[here, :], kv[0, j]) * score_scale
            if j == reach:
                score = jnp.where(col <= row, score, -1e30)
            else:
                score = jnp.where(s >= reach - j, score, -1e30)
                if j == 0:
                    score = jnp.where(col > row, score, -1e30)
            scores.append(score)
        top = scores[0]
        for score in scores[1:]:
            top = jnp.maximum(top, score)
        top = jnp.max(top, axis=1, keepdims=True)
        exps = [jnp.exp(score - top) for score in scores]
        mass = exps[0]
        for e in exps[1:]:
            mass = mass + e
        inverse = 1.0 / jnp.sum(mass, axis=1, keepdims=True)
        for j in range(reach + 1):
            p = exps[j] * inverse
            probs[here, j * tokens : (j + 1) * tokens] = p
            low[here, j * tokens : (j + 1) * tokens] = p.astype(bf16)

    pass_halo(1)
    relay_second(2)
    for copy in part:
        copy.wait_recv()
    for i in (3, 4):
        for slot in (ACROSS, DIAG):
            to_far(i, slot).start()
    grad_heads = own_part[...]
    for r in range(1, PEERS):
        grad_heads = grad_heads + partial_in[r - 1].astype(f32)
    grad_heads = grad_heads.astype(bf16)

    for j in range(reach + 1):
        parts[1, j] = dot_cols(low[:, j * tokens : (j + 1) * tokens], grad_heads).astype(bf16)
    swap = remote(C_SWAP, parts.at[1 - core], parts_in, s, sib)

    @pl.when(core == 0)
    def _():
        swap.start()

    back_copies = [
        remote(C_BACK + d - 1, back.at[reach - d], back_in.at[d - 1], s - d, h)
        for d in range(1, reach + 1)
    ]

    def send_back(which):
        @pl.when(core == which)
        def _():
            swap.wait_recv()
            for d in range(reach, -1, -1):
                j = reach - d
                both = parts[which, j].astype(f32) + parts_in[j].astype(f32)
                if d == 0:
                    total[...] = both
                else:
                    back[j] = both.astype(bf16)

                    @pl.when(s >= d)
                    def _():
                        back_copies[d - 1].start()

    get_halo(1)
    for i in range(ROW_CHUNKS):
        if i == ROW_CHUNKS // 2:
            send_back(1)
        here = pl.ds(i * rows, rows)
        block = grad_heads[i * rows : (i + 1) * rows]
        weighted = []
        products = []
        for j in range(reach + 1):
            p = probs[here, j * tokens : (j + 1) * tokens]
            dp = dot_rows(block, kv[1, j])
            products.append(dp)
            weighted.append(p * dp)
        delta = weighted[0]
        for w in weighted[1:]:
            delta = delta + w
        delta = jnp.sum(delta, axis=1, keepdims=True)
        for j in range(reach + 1):
            p = probs[here, j * tokens : (j + 1) * tokens]
            ds[here, j * tokens : (j + 1) * tokens] = (p * (products[j] - delta)).astype(bf16)
    for j in range(reach + 1):
        parts[0, j] = (
            dot_cols(ds[:, j * tokens : (j + 1) * tokens], query[...]) * score_scale
        ).astype(bf16)

    @pl.when(core == 1)
    def _():
        swap.start()

    grad_query = jnp.zeros((tokens, HEAD), f32)
    for j in range(reach + 1):
        grad_query = grad_query + jnp.dot(
            ds[:, j * tokens : (j + 1) * tokens], kv[0, j], preferred_element_type=f32)
    grads[0, 0] = (grad_query * score_scale).astype(bf16)

    send_back(0)

    def share(t):
        return [
            remote(C_GRAD + 3 * t + r - 1, grads.at[t, 0], grads.at[t, r], s, peers[r])
            for r in range(1, PEERS)
        ]

    share_query = share(0)
    for copy in share_query:
        copy.start()
    relay_first(3)

    for copy in share_query:
        copy.wait_recv()
    load_own[0].wait()
    to_sib(1).wait_recv()
    arrived(2)
    chunk = width // 7

    def product(t, first):
        right = jnp.concatenate([grads[t, r] for r in range(PEERS)], axis=1)
        left = jnp.concatenate(
            [weights[t, r, first : first + chunk] for r in range(PEERS)], axis=1)
        return dot_rows(left, right)

    for first in range(0, width, chunk):
        acc[first : first + chunk] = product(0, first)
    relay_first(4)
    for d in range(1, reach + 1):
        @pl.when(s + d < seqs)
        def _():
            back_copies[d - 1].wait_recv()
            total[...] += back_in[d - 1].astype(f32)
    grads[1, 0] = total[...].astype(bf16)
    share_pair = share(1)
    for copy in share_pair:
        copy.start()

    load_own[1].wait()
    to_sib(2).wait_recv()
    arrived(3)
    arrived(4)
    for copy in share_pair:
        copy.wait_recv()
    for first in range(0, width, chunk):
        here = slice(first, first + chunk)
        out[here] = (acc[here] + product(1, first)).astype(bf16)

    for copy in part + share_query + share_pair + [swap]:
        copy.wait_send()
    for t in range(3):
        to_sib(t).wait_send()
    for i in range(5):
        for slot in (ACROSS, DIAG):
            to_far(i, slot).wait_send()
            for step in steps_of(i):
                relay(i, slot, step).wait_send()
    for d in range(1, reach + 1):
        @pl.when(s + d < seqs)
        def _():
            halo[d - 1].wait_send()

        @pl.when(s >= d)
        def _():
            passed[d - 1].wait_send()
            back_copies[d - 1].wait_send()


def fused(seqs, query, keys, values, d_out, w_out, w_query, w_key, w_value):
    tokens, width = d_out.shape
    wide = -(-width // 128) * 128
    span = (NBR + 1) * tokens
    bf16, f32 = jnp.bfloat16, jnp.float32
    vmem = pl.BlockSpec(memory_space=pltpu.VMEM)
    hbm = pl.BlockSpec(memory_space=pltpu.HBM)
    return pl.pallas_call(
        functools.partial(kernel, seqs),
        out_shape=jax.ShapeDtypeStruct((width, tokens), bf16),
        in_specs=[hbm] * 8,
        out_specs=vmem,
        scratch_shapes=[
            pltpu.VMEM(w_query.shape, bf16),
            pltpu.VMEM(w_key.shape, bf16),
            pltpu.VMEM(w_out.shape, bf16),
            pltpu.VMEM((wide, tokens), bf16),
            pltpu.VMEM((PEERS, HEAD, wide), bf16),
            pltpu.VMEM((PEERS, HEAD, wide), bf16),
            pltpu.VMEM((tokens, HEAD), bf16),
            pltpu.VMEM((2, NBR + 1, tokens, HEAD), bf16),
            pltpu.VMEM((tokens, span), f32),
            pltpu.VMEM((tokens, span), bf16),
            pltpu.VMEM((tokens, span), bf16),
            pltpu.VMEM((tokens, HEAD), f32),
            pltpu.VMEM((PEERS - 1, tokens, HEAD), bf16),
            pltpu.VMEM((PEERS - 1, tokens, HEAD), bf16),
            pltpu.VMEM((2, NBR + 1, tokens, HEAD), bf16),
            pltpu.VMEM((NBR + 1, tokens, HEAD), bf16),
            pltpu.VMEM((NBR, tokens, HEAD), bf16),
            pltpu.VMEM((NBR, tokens, HEAD), bf16),
            pltpu.VMEM((2, PEERS, tokens, HEAD), bf16),
            pltpu.VMEM((2, PEERS, width, HEAD), bf16),
            pltpu.VMEM((tokens, HEAD), f32),
            pltpu.VMEM((width, tokens), f32),
            pltpu.SemaphoreType.DMA((C_END,)),
            pltpu.SemaphoreType.DMA((C_END,)),
            pltpu.SemaphoreType.DMA((9,)),
        ],
        compiler_params=pltpu.CompilerParams(
            collective_id=0, has_side_effects=True, vmem_limit_bytes=48 * 1024 * 1024,
        ),
    )(*(
        pltpu.with_memory_space_constraint(x, pltpu.HBM)
        for x in (query, keys, values, d_out.T, w_out, w_query, w_key, w_value)
    )).T


def solution(mesh):
    in_specs = (
        P("seq", "head"),
        P("seq", "head"),
        P("seq", "head"),
        P("seq", "head"),
        P("head", None),
        P(None, "head"),
        P(None, "head"),
        P(None, "head"),
    )
    out_specs = P("seq", "head")
    seqs, peers = mesh.shape["seq"], mesh.shape["head"]

    def local(query, keys, values, d_out, w_out, w_query, w_key, w_value):
        args = (query, keys, values, d_out, w_out, w_query, w_key, w_value)
        tokens, width = d_out.shape
        fits = peers == PEERS and seqs % 4 == 0 and query.shape[1] == HEAD
        fits = fits and tokens * NBR == WINDOW and width % (64 * 7) == 0
        return fused(seqs, *args) if fits else body(*args)

    return jax.shard_map(local, mesh=mesh, in_specs=in_specs, out_specs=out_specs, check_vma=False)
```

```python
import functools

import jax
import jax.numpy as jnp
from jax import lax
from jax.experimental import pallas as pl
from jax.experimental.pallas import tpu as pltpu
from jax.sharding import PartitionSpec as P

WINDOW = 1024
NBR = 4
HEAD = 128


score_scale = 168.0 ** (-0.5)


def from_behind(block, axis, distance):
    devices = range(lax.axis_size(axis))
    route = [(i - distance, i) for i in devices if i - distance in devices]
    return lax.ppermute(block, axis, route)


def dot_rows(left, right):
    return lax.dot_general(
        left, right, (((1,), (1,)), ((), ())), preferred_element_type=jnp.float32
    )


def dot_cols(left, right):
    return lax.dot_general(
        left, right, (((0,), (0,)), ((), ())), preferred_element_type=jnp.float32
    )


def band_backward(query_block, key_band, value_band, grad_block, query_start, key_start):
    length = query_block.shape[0]
    span = key_band.shape[0]
    query_pos = query_start + jnp.arange(length, dtype=jnp.int32)
    key_pos = key_start + jnp.arange(span, dtype=jnp.int32)
    offset = query_pos[:, None] - key_pos[None, :]
    allowed = (key_pos[None, :] >= 0) & (offset >= 0) & (offset < WINDOW)
    scores = dot_rows(query_block, key_band) * score_scale
    masked = jnp.where(allowed, scores, -1e30)
    top = jnp.max(masked, axis=1, keepdims=True)
    weights = jnp.where(allowed, jnp.exp(masked - top), 0.0)
    probs = weights / jnp.sum(weights, axis=1, keepdims=True)
    probs_low = probs.astype(jnp.bfloat16)
    grad_probs = dot_rows(grad_block, value_band)
    delta = jnp.sum(probs * grad_probs, axis=1, keepdims=True)
    grad_scores = (probs * (grad_probs - delta)).astype(jnp.bfloat16)
    grad_query = (
        jnp.dot(grad_scores, key_band, preferred_element_type=jnp.float32) * score_scale
    ).astype(jnp.bfloat16)
    grad_keys = (dot_cols(grad_scores, query_block) * score_scale).astype(jnp.bfloat16)
    grad_values = dot_cols(probs_low, grad_block).astype(jnp.bfloat16)
    return (grad_query, grad_keys, grad_values)


def body(query, keys, values, d_out, w_out, w_query, w_key, w_value):
    length = query.shape[0]
    seq_index = lax.axis_index("seq")
    gathered = lax.all_gather(d_out, "head", axis=1, tiled=True)
    grad_heads = dot_rows(gathered, w_out).astype(jnp.bfloat16)
    reach = NBR
    key_blocks = []
    value_blocks = []
    for distance in range(reach, 0, -1):
        far_keys, far_values = from_behind((keys, values), "seq", distance)
        key_blocks.append(far_keys)
        value_blocks.append(far_values)
    key_band = jnp.concatenate(key_blocks + [keys], axis=0)
    value_band = jnp.concatenate(value_blocks + [values], axis=0)
    query_start = seq_index * length
    grad_query, key_parts, value_parts = band_backward(
        query, key_band, value_band, grad_heads, query_start, query_start - reach * length
    )
    key_total = key_parts[reach * length :].astype(jnp.float32)
    value_total = value_parts[reach * length :].astype(jnp.float32)
    for distance in range(1, reach + 1):
        first = (reach - distance) * length
        outgoing = (key_parts[first : first + length], value_parts[first : first + length])
        back_keys, back_values = from_behind((outgoing[0], outgoing[1]), "seq", -distance)
        key_total = key_total + back_keys.astype(jnp.float32)
        value_total = value_total + back_values.astype(jnp.float32)
    grad_keys = key_total.astype(jnp.bfloat16)
    grad_values = value_total.astype(jnp.bfloat16)
    summed = dot_rows(w_query, grad_query)
    summed = summed + dot_rows(w_key, grad_keys)
    summed = summed + dot_rows(w_value, grad_values)
    reduced = lax.psum_scatter(
        summed.astype(jnp.bfloat16), "head", scatter_dimension=0, tiled=True
    ).astype(jnp.float32)
    return reduced.T.astype(jnp.bfloat16)


PEERS = 4
SIB, ACROSS, DIAG = 1, 2, 3
ROW_CHUNKS = 4
MESH = pl.DeviceIdType.MESH

C_SIB = 0
C_FAR = C_SIB + 3
C_RELAY = C_FAR + 10
C_HALO = C_RELAY + 30
C_PASS = C_HALO + NBR
C_PART = C_PASS + NBR
C_SWAP = C_PART + 3
C_BACK = C_SWAP + 1
C_GRAD = C_BACK + NBR
C_END = C_GRAD + 6


def kernel(
    seqs, query_in, keys_in, values_in, d_out, w_out, w_query, w_key, w_value, out,
    wq_all, wkv_all, wout_all, d_own, w_cut, w_heads, query, kv, probs, products, low, ds,
    own_part, partial, partial_in, parts, parts_in, back, back_in, grads, weights, total, acc,
    send, recv, local,
):
    s = lax.axis_index("seq")
    h = lax.axis_index("head")
    core = lax.rem(h, 2)
    sib = h + 1 - 2 * core
    across = lax.rem(h + 2, 4)
    diag = lax.rem(sib + 2, 4)
    peers = (None, sib, across, diag)
    y = lax.rem(s, 2)
    z = lax.rem(s // 2, 2)
    pair_y = s + 1 - 2 * y
    pair_z = s + 2 - 4 * z
    quarter = 2 * y + z
    quarter_z = 2 * y + 1 - z
    quarter_y = 2 - 2 * y + z
    width, tokens = out.shape
    wide = d_own.shape[0]
    reach = NBR
    f32, bf16 = jnp.float32, jnp.bfloat16

    barrier = pltpu.get_barrier_semaphore()
    for r in range(1, PEERS):
        pl.semaphore_signal(barrier, inc=1, device_id=(s, peers[r]), device_id_type=MESH)
    for d in range(1, reach + 1):
        @pl.when(s >= d)
        def _():
            pl.semaphore_signal(barrier, inc=1, device_id=(s - d, h), device_id_type=MESH)

        @pl.when(s + d < seqs)
        def _():
            pl.semaphore_signal(barrier, inc=1, device_id=(s + d, h), device_id_type=MESH)

    def remote(index, src, dst, seq, head):
        return pltpu.make_async_remote_copy(
            src_ref=src, dst_ref=dst, send_sem=send.at[index], recv_sem=recv.at[index],
            device_id=(seq, head), device_id_type=MESH,
        )

    load_wout = pltpu.make_async_copy(w_out, wout_all, local.at[0])
    load_dout = pltpu.make_async_copy(d_out, d_own.at[pl.ds(0, width)], local.at[1])
    load_keys = pltpu.make_async_copy(keys_in, kv.at[0, reach], local.at[2])
    load_values = pltpu.make_async_copy(values_in, kv.at[1, reach], local.at[3])
    load_query = pltpu.make_async_copy(query_in, query, local.at[4])
    load_wq = pltpu.make_async_copy(w_query, wq_all, local.at[5])
    load_wk = pltpu.make_async_copy(w_key, wkv_all, local.at[6])
    load_wv = pltpu.make_async_copy(w_value, wkv_all, local.at[6])
    for copy in (load_wout, load_keys, load_values, load_dout, load_query):
        copy.start()

    for d in range(1, reach + 1):
        @pl.when(s < d)
        def _():
            kv[0, reach - d] = jnp.zeros((tokens, HEAD), bf16)
            kv[1, reach - d] = jnp.zeros((tokens, HEAD), bf16)

    d_own[width:wide] = jnp.zeros((wide - width, tokens), bf16)

    pad = jnp.zeros((HEAD, wide - width), bf16)
    load_wout.wait()
    load_wq.start()

    @pl.when(core == 0)
    def _():
        load_wk.start()

    @pl.when(core == 1)
    def _():
        load_wv.start()

    for b in range(PEERS):
        shift = b * width % 128
        first = b * width - shift
        room = min(width + 128, wout_all.shape[1] - first)
        cut = wout_all[:, first : first + room][:, shift : shift + width]
        cut = jnp.concatenate([cut, pad], axis=1)
        w_cut[b] = cut

        @pl.when(h == b)
        def _():
            w_heads[0] = cut

    behind = jnp.minimum(s, reach)
    ahead = jnp.minimum(seqs - 1 - s, reach)
    pl.semaphore_wait(barrier, PEERS - 1 + behind + ahead)

    piece = (HEAD // 8, HEAD // 8, width // 4, width // 4, width // 4)
    slab_of = (0, 0, 1, 2, 2)
    slabs = (w_heads, weights.at[0], weights.at[1])
    alls = (None, wq_all, wkv_all)

    def start_of(i, index):
        if slab_of[i] == 0:
            return (index * 2 + i) * piece[i]
        if slab_of[i] == 1:
            return index * piece[i]
        return (2 * y + i - 3) * piece[i]

    def rows_of(i, index):
        return pl.ds(pl.multiple_of(start_of(i, index), 16), piece[i])

    def to_sib(t):
        if t == 0:
            src = w_cut.at[sib]
        else:
            src = alls[t].at[pl.ds(pl.multiple_of(sib * width, 16), width)]
        return remote(C_SIB + t, src, slabs[t].at[SIB], s, sib)

    def to_far(i, slot):
        peer = peers[slot]
        t = slab_of[i]
        if t == 0:
            src = w_cut.at[peer, rows_of(i, quarter)]
        else:
            first = peer * width + start_of(i, quarter)
            src = alls[t].at[pl.ds(pl.multiple_of(first, 16), piece[i])]
        dst = slabs[t].at[slot, rows_of(i, quarter)]
        return remote(C_FAR + 2 * i + slot - ACROSS, src, dst, s, peer)

    def relay(i, slot, step):
        if step < 2:
            index, target = quarter, (pair_z, pair_y)[step]
        elif slab_of[i] == 0 and slot == DIAG:
            index, target = quarter_y, pair_z
        else:
            index, target = quarter_z, pair_y
        block = slabs[slab_of[i]].at[slot, rows_of(i, index)]
        number = 6 * i + 3 * (slot - ACROSS) + step
        return remote(C_RELAY + number, block, block, target, h)

    def steps_of(i):
        return (1,) if slab_of[i] == 2 else (0, 1, 2)

    def relay_first(i):
        for slot in (ACROSS, DIAG):
            to_far(i, slot).wait_recv()
            for step in steps_of(i)[:2]:
                relay(i, slot, step).start()

    def relay_second(i):
        for slot in (ACROSS, DIAG):
            over_y = slab_of[i] == 0 and slot == DIAG
            relay(i, slot, 1 if over_y else 0).wait_recv()
            relay(i, slot, 2).start()

    def arrived(i):
        for slot in (ACROSS, DIAG):
            over_y = slab_of[i] == 0 and slot == DIAG
            relay(i, slot, 0 if over_y else 1).wait_recv()
            if slab_of[i] < 2:
                relay(i, slot, 2).wait_recv()

    for i in (0, 1):
        for slot in (ACROSS, DIAG):
            to_far(i, slot).start()
    to_sib(0).start()
    load_keys.wait()
    load_values.wait()
    halo = [
        remote(C_HALO + d - 1, kv.at[core, reach], kv.at[core, reach - d], s + d, h)
        for d in range(1, reach + 1)
    ]
    passed = [
        remote(C_PASS + d - 1, kv.at[core, reach - d], kv.at[core, reach - d], s, sib)
        for d in range(1, reach + 1)
    ]

    def send_halo(which):
        for d in range(1, reach + 1):
            @pl.when((core == which) & (s + d < seqs))
            def _():
                halo[d - 1].start()

    def pass_halo(which):
        for d in range(1, reach + 1):
            @pl.when((core == which) & (s >= d))
            def _():
                halo[d - 1].wait_recv()
                passed[d - 1].start()

    def get_halo(which):
        for d in range(1, reach + 1):
            @pl.when((core != which) & (s >= d))
            def _():
                passed[d - 1].wait_recv()

    send_halo(0)
    load_dout.wait()
    load_wq.wait()
    load_wk.wait()
    load_own = []
    for t in (1, 2):
        rows_own = pl.ds(pl.multiple_of(h * width, 16), width)
        load_own.append(
            pltpu.make_async_copy(alls[t].at[rows_own], slabs[t].at[0], local.at[6 + t]))
    relay_first(0)
    relay_first(1)
    for slot in (ACROSS, DIAG):
        to_far(2, slot).start()

    to_sib(0).wait_recv()
    rows = tokens // ROW_CHUNKS
    both_heads = 2 * HEAD
    d_all = d_own[...]
    near = w_heads[0:2].reshape(both_heads, wide)
    result = jnp.dot(near, d_all, preferred_element_type=f32).T
    own_part[...] = result[:, :HEAD]
    partial[SIB - 1] = result[:, HEAD:].astype(bf16)
    part = [
        remote(C_PART + r - 1, partial.at[r - 1], partial_in.at[r - 1], s, peers[r])
        for r in range(1, PEERS)
    ]
    part[SIB - 1].start()
    relay_second(0)
    relay_second(1)
    send_halo(1)
    pass_halo(0)
    arrived(0)
    arrived(1)
    far = w_heads[2:4].reshape(both_heads, wide)
    result = jnp.dot(far, d_all, preferred_element_type=f32).T.astype(bf16)
    partial[ACROSS - 1] = result[:, :HEAD]
    partial[DIAG - 1] = result[:, HEAD:]
    part[ACROSS - 1].start()
    part[DIAG - 1].start()
    for copy in load_own:
        copy.start()
    for t in (1, 2):
        to_sib(t).start()
    relay_first(2)
    load_query.wait()
    get_halo(0)

    row = lax.broadcasted_iota(jnp.int32, (tokens, tokens), 0)
    col = lax.broadcasted_iota(jnp.int32, (tokens, tokens), 1)
    query_all = query[...]
    for j in range(reach + 1):
        score = dot_rows(query_all, kv[0, j]) * score_scale
        if j == reach:
            score = jnp.where(col <= row, score, -1e30)
        else:
            score = jnp.where(s >= reach - j, score, -1e30)
            if j == 0:
                score = jnp.where(col > row, score, -1e30)
        probs[:, j * tokens : (j + 1) * tokens] = score
    for i in range(ROW_CHUNKS):
        here = pl.ds(i * rows, rows)
        score = probs[here, :]
        exps = jnp.exp(score - jnp.max(score, axis=1, keepdims=True))
        p = exps * (1.0 / jnp.sum(exps, axis=1, keepdims=True))
        probs[here, :] = p
        low[here, :] = p.astype(bf16)

    pass_halo(1)
    relay_second(2)
    for copy in part:
        copy.wait_recv()
    for i in (3, 4):
        for slot in (ACROSS, DIAG):
            to_far(i, slot).start()
    grad_heads = own_part[...]
    for r in range(1, PEERS):
        grad_heads = grad_heads + partial_in[r - 1].astype(f32)
    grad_heads = grad_heads.astype(bf16)

    for j in range(reach + 1):
        parts[1, j] = dot_cols(low[:, j * tokens : (j + 1) * tokens], grad_heads).astype(bf16)
    swap = remote(C_SWAP, parts.at[1 - core], parts_in, s, sib)

    @pl.when(core == 0)
    def _():
        swap.start()

    back_copies = [
        remote(C_BACK + d - 1, back.at[reach - d], back_in.at[d - 1], s - d, h)
        for d in range(1, reach + 1)
    ]

    def send_back(which):
        @pl.when(core == which)
        def _():
            swap.wait_recv()
            for d in range(reach, -1, -1):
                j = reach - d
                both = parts[which, j].astype(f32) + parts_in[j].astype(f32)
                if d == 0:
                    total[...] = both
                else:
                    back[j] = both.astype(bf16)

                    @pl.when(s >= d)
                    def _():
                        back_copies[d - 1].start()

    get_halo(1)
    for j in range(reach + 1):
        products[:, j * tokens : (j + 1) * tokens] = dot_rows(grad_heads, kv[1, j])
    send_back(1)
    for i in range(ROW_CHUNKS):
        here = pl.ds(i * rows, rows)
        p = probs[here, :]
        dp = products[here, :]
        delta = jnp.sum(p * dp, axis=1, keepdims=True)
        ds[here, :] = (p * (dp - delta)).astype(bf16)
    for j in range(reach + 1):
        parts[0, j] = (
            dot_cols(ds[:, j * tokens : (j + 1) * tokens], query[...]) * score_scale
        ).astype(bf16)

    @pl.when(core == 1)
    def _():
        swap.start()

    grad_query = jnp.zeros((tokens, HEAD), f32)
    for j in range(reach + 1):
        grad_query = grad_query + jnp.dot(
            ds[:, j * tokens : (j + 1) * tokens], kv[0, j], preferred_element_type=f32)
    grads[0, 0] = (grad_query * score_scale).astype(bf16)

    send_back(0)

    def share(t):
        return [
            remote(C_GRAD + 3 * t + r - 1, grads.at[t, 0], grads.at[t, r], s, peers[r])
            for r in range(1, PEERS)
        ]

    share_query = share(0)
    for copy in share_query:
        copy.start()
    relay_first(3)

    for copy in share_query:
        copy.wait_recv()
    load_own[0].wait()
    to_sib(1).wait_recv()
    arrived(2)
    chunk = width // 2

    def product(t, slots, first):
        right = jnp.concatenate([grads[t, r] for r in slots], axis=1)
        left = jnp.concatenate([weights[t, r, first : first + chunk] for r in slots], axis=1)
        return dot_rows(left, right)

    for first in range(0, width, chunk):
        acc[first : first + chunk] = product(0, range(PEERS), first)
    relay_first(4)
    for d in range(1, reach + 1):
        @pl.when(s + d < seqs)
        def _():
            back_copies[d - 1].wait_recv()
            total[...] += back_in[d - 1].astype(f32)
    grads[1, 0] = total[...].astype(bf16)
    share_pair = share(1)
    for copy in share_pair:
        copy.start()

    load_own[1].wait()
    to_sib(2).wait_recv()
    share_pair[SIB - 1].wait_recv()
    for first in range(0, width, chunk):
        acc[first : first + chunk] += product(1, (0, SIB), first)
    arrived(3)
    arrived(4)
    for copy in share_pair[SIB:]:
        copy.wait_recv()
    for first in range(0, width, chunk):
        here = slice(first, first + chunk)
        out[here] = (acc[here] + product(1, (ACROSS, DIAG), first)).astype(bf16)

    for copy in part + share_query + share_pair + [swap]:
        copy.wait_send()
    for t in range(3):
        to_sib(t).wait_send()
    for i in range(5):
        for slot in (ACROSS, DIAG):
            to_far(i, slot).wait_send()
            for step in steps_of(i):
                relay(i, slot, step).wait_send()
    for d in range(1, reach + 1):
        @pl.when(s + d < seqs)
        def _():
            halo[d - 1].wait_send()

        @pl.when(s >= d)
        def _():
            passed[d - 1].wait_send()
            back_copies[d - 1].wait_send()


def fused(seqs, query, keys, values, d_out, w_out, w_query, w_key, w_value):
    tokens, width = d_out.shape
    wide = -(-width // 128) * 128
    span = (NBR + 1) * tokens
    bf16, f32 = jnp.bfloat16, jnp.float32
    vmem = pl.BlockSpec(memory_space=pltpu.VMEM)
    hbm = pl.BlockSpec(memory_space=pltpu.HBM)
    return pl.pallas_call(
        functools.partial(kernel, seqs),
        out_shape=jax.ShapeDtypeStruct((width, tokens), bf16),
        in_specs=[hbm] * 8,
        out_specs=vmem,
        scratch_shapes=[
            pltpu.VMEM(w_query.shape, bf16),
            pltpu.VMEM(w_key.shape, bf16),
            pltpu.VMEM(w_out.shape, bf16),
            pltpu.VMEM((wide, tokens), bf16),
            pltpu.VMEM((PEERS, HEAD, wide), bf16),
            pltpu.VMEM((PEERS, HEAD, wide), bf16),
            pltpu.VMEM((tokens, HEAD), bf16),
            pltpu.VMEM((2, NBR + 1, tokens, HEAD), bf16),
            pltpu.VMEM((tokens, span), f32),
            pltpu.VMEM((tokens, span), f32),
            pltpu.VMEM((tokens, span), bf16),
            pltpu.VMEM((tokens, span), bf16),
            pltpu.VMEM((tokens, HEAD), f32),
            pltpu.VMEM((PEERS - 1, tokens, HEAD), bf16),
            pltpu.VMEM((PEERS - 1, tokens, HEAD), bf16),
            pltpu.VMEM((2, NBR + 1, tokens, HEAD), bf16),
            pltpu.VMEM((NBR + 1, tokens, HEAD), bf16),
            pltpu.VMEM((NBR, tokens, HEAD), bf16),
            pltpu.VMEM((NBR, tokens, HEAD), bf16),
            pltpu.VMEM((2, PEERS, tokens, HEAD), bf16),
            pltpu.VMEM((2, PEERS, width, HEAD), bf16),
            pltpu.VMEM((tokens, HEAD), f32),
            pltpu.VMEM((width, tokens), f32),
            pltpu.SemaphoreType.DMA((C_END,)),
            pltpu.SemaphoreType.DMA((C_END,)),
            pltpu.SemaphoreType.DMA((9,)),
        ],
        compiler_params=pltpu.CompilerParams(
            collective_id=0, has_side_effects=True, vmem_limit_bytes=48 * 1024 * 1024,
        ),
    )(*(
        pltpu.with_memory_space_constraint(x, pltpu.HBM)
        for x in (query, keys, values, d_out.T, w_out, w_query, w_key, w_value)
    )).T


def solution(mesh):
    in_specs = (
        P("seq", "head"),
        P("seq", "head"),
        P("seq", "head"),
        P("seq", "head"),
        P("head", None),
        P(None, "head"),
        P(None, "head"),
        P(None, "head"),
    )
    out_specs = P("seq", "head")
    seqs, peers = mesh.shape["seq"], mesh.shape["head"]

    def local(query, keys, values, d_out, w_out, w_query, w_key, w_value):
        args = (query, keys, values, d_out, w_out, w_query, w_key, w_value)
        tokens, width = d_out.shape
        fits = peers == PEERS and seqs % 4 == 0 and query.shape[1] == HEAD
        fits = fits and tokens * NBR == WINDOW and width % 64 == 0
        return fused(seqs, *args) if fits else body(*args)

    return jax.shard_map(local, mesh=mesh, in_specs=in_specs, out_specs=out_specs, check_vma=False)
```

```python
import functools

import jax
import jax.numpy as jnp
from jax import lax
from jax.experimental import pallas as pl
from jax.experimental.pallas import tpu as pltpu
from jax.sharding import PartitionSpec as P

WINDOW = 1024
NBR = 4
HEAD = 128


score_scale = 168.0 ** (-0.5)


def from_behind(block, axis, distance):
    devices = range(lax.axis_size(axis))
    route = [(i - distance, i) for i in devices if i - distance in devices]
    return lax.ppermute(block, axis, route)


def dot_rows(left, right):
    return lax.dot_general(
        left, right, (((1,), (1,)), ((), ())), preferred_element_type=jnp.float32
    )


def dot_cols(left, right):
    return lax.dot_general(
        left, right, (((0,), (0,)), ((), ())), preferred_element_type=jnp.float32
    )


def band_backward(query_block, key_band, value_band, grad_block, query_start, key_start):
    length = query_block.shape[0]
    span = key_band.shape[0]
    query_pos = query_start + jnp.arange(length, dtype=jnp.int32)
    key_pos = key_start + jnp.arange(span, dtype=jnp.int32)
    offset = query_pos[:, None] - key_pos[None, :]
    allowed = (key_pos[None, :] >= 0) & (offset >= 0) & (offset < WINDOW)
    scores = dot_rows(query_block, key_band) * score_scale
    masked = jnp.where(allowed, scores, -1e30)
    top = jnp.max(masked, axis=1, keepdims=True)
    weights = jnp.where(allowed, jnp.exp(masked - top), 0.0)
    probs = weights / jnp.sum(weights, axis=1, keepdims=True)
    probs_low = probs.astype(jnp.bfloat16)
    grad_probs = dot_rows(grad_block, value_band)
    delta = jnp.sum(probs * grad_probs, axis=1, keepdims=True)
    grad_scores = (probs * (grad_probs - delta)).astype(jnp.bfloat16)
    grad_query = (
        jnp.dot(grad_scores, key_band, preferred_element_type=jnp.float32) * score_scale
    ).astype(jnp.bfloat16)
    grad_keys = (dot_cols(grad_scores, query_block) * score_scale).astype(jnp.bfloat16)
    grad_values = dot_cols(probs_low, grad_block).astype(jnp.bfloat16)
    return (grad_query, grad_keys, grad_values)


def body(query, keys, values, d_out, w_out, w_query, w_key, w_value):
    length = query.shape[0]
    seq_index = lax.axis_index("seq")
    gathered = lax.all_gather(d_out, "head", axis=1, tiled=True)
    grad_heads = dot_rows(gathered, w_out).astype(jnp.bfloat16)
    reach = NBR
    key_blocks = []
    value_blocks = []
    for distance in range(reach, 0, -1):
        far_keys, far_values = from_behind((keys, values), "seq", distance)
        key_blocks.append(far_keys)
        value_blocks.append(far_values)
    key_band = jnp.concatenate(key_blocks + [keys], axis=0)
    value_band = jnp.concatenate(value_blocks + [values], axis=0)
    query_start = seq_index * length
    grad_query, key_parts, value_parts = band_backward(
        query, key_band, value_band, grad_heads, query_start, query_start - reach * length
    )
    key_total = key_parts[reach * length :].astype(jnp.float32)
    value_total = value_parts[reach * length :].astype(jnp.float32)
    for distance in range(1, reach + 1):
        first = (reach - distance) * length
        outgoing = (key_parts[first : first + length], value_parts[first : first + length])
        back_keys, back_values = from_behind((outgoing[0], outgoing[1]), "seq", -distance)
        key_total = key_total + back_keys.astype(jnp.float32)
        value_total = value_total + back_values.astype(jnp.float32)
    grad_keys = key_total.astype(jnp.bfloat16)
    grad_values = value_total.astype(jnp.bfloat16)
    summed = dot_rows(w_query, grad_query)
    summed = summed + dot_rows(w_key, grad_keys)
    summed = summed + dot_rows(w_value, grad_values)
    reduced = lax.psum_scatter(
        summed.astype(jnp.bfloat16), "head", scatter_dimension=0, tiled=True
    ).astype(jnp.float32)
    return reduced.T.astype(jnp.bfloat16)


PEERS = 4
SIB, ACROSS, DIAG = 1, 2, 3
ROW_CHUNKS = 4
MESH = pl.DeviceIdType.MESH

C_SIB = 0
C_FAR = C_SIB + 3
C_RELAY = C_FAR + 10
C_HALO = C_RELAY + 30
C_PASS = C_HALO + NBR
C_PART = C_PASS + NBR
C_SWAP = C_PART + 3
C_BACK = C_SWAP + NBR + 1
C_GRAD = C_BACK + NBR
C_END = C_GRAD + 6


def kernel(
    seqs, query_in, keys_in, values_in, d_out, w_out, w_query, w_key, w_value, out,
    wq_all, wkv_all, wout_all, d_own, w_cut, w_heads, query, kv, probs, products, low, ds,
    own_part, partial, partial_in, parts, parts_in, back, back_in, grads, weights, total, acc,
    send, recv, local,
):
    s = lax.axis_index("seq")
    h = lax.axis_index("head")
    core = lax.rem(h, 2)
    sib = h + 1 - 2 * core
    across = lax.rem(h + 2, 4)
    diag = lax.rem(sib + 2, 4)
    peers = (None, sib, across, diag)
    y = lax.rem(s, 2)
    z = lax.rem(s // 2, 2)
    pair_y = s + 1 - 2 * y
    pair_z = s + 2 - 4 * z
    quarter = 2 * y + z
    quarter_z = 2 * y + 1 - z
    quarter_y = 2 - 2 * y + z
    width, tokens = out.shape
    wide = d_own.shape[0]
    reach = NBR
    f32, bf16 = jnp.float32, jnp.bfloat16

    barrier = pltpu.get_barrier_semaphore()
    for r in range(1, PEERS):
        pl.semaphore_signal(barrier, inc=1, device_id=(s, peers[r]), device_id_type=MESH)
    for d in range(1, reach + 1):
        @pl.when(s >= d)
        def _():
            pl.semaphore_signal(barrier, inc=1, device_id=(s - d, h), device_id_type=MESH)

        @pl.when(s + d < seqs)
        def _():
            pl.semaphore_signal(barrier, inc=1, device_id=(s + d, h), device_id_type=MESH)

    def remote(index, src, dst, seq, head):
        return pltpu.make_async_remote_copy(
            src_ref=src, dst_ref=dst, send_sem=send.at[index], recv_sem=recv.at[index],
            device_id=(seq, head), device_id_type=MESH,
        )

    load_wout = pltpu.make_async_copy(w_out, wout_all, local.at[0])
    load_dout = pltpu.make_async_copy(d_out, d_own.at[pl.ds(0, width)], local.at[1])
    load_keys = pltpu.make_async_copy(keys_in, kv.at[0, reach], local.at[2])
    load_values = pltpu.make_async_copy(values_in, kv.at[1, reach], local.at[3])
    load_query = pltpu.make_async_copy(query_in, query, local.at[4])
    load_wq = pltpu.make_async_copy(w_query, wq_all, local.at[5])
    load_wk = pltpu.make_async_copy(w_key, wkv_all, local.at[6])
    load_wv = pltpu.make_async_copy(w_value, wkv_all, local.at[6])
    for copy in (load_wout, load_keys, load_values, load_dout, load_query):
        copy.start()

    for d in range(1, reach + 1):
        @pl.when(s < d)
        def _():
            kv[0, reach - d] = jnp.zeros((tokens, HEAD), bf16)
            kv[1, reach - d] = jnp.zeros((tokens, HEAD), bf16)

    d_own[width:wide] = jnp.zeros((wide - width, tokens), bf16)

    pad = jnp.zeros((HEAD, wide - width), bf16)
    load_wout.wait()
    load_wq.start()

    @pl.when(core == 0)
    def _():
        load_wk.start()

    @pl.when(core == 1)
    def _():
        load_wv.start()

    for b in range(PEERS):
        shift = b * width % 128
        first = b * width - shift
        room = min(width + 128, wout_all.shape[1] - first)
        cut = wout_all[:, first : first + room][:, shift : shift + width]
        cut = jnp.concatenate([cut, pad], axis=1)
        w_cut[b] = cut

        @pl.when(h == b)
        def _():
            w_heads[0] = cut

    behind = jnp.minimum(s, reach)
    ahead = jnp.minimum(seqs - 1 - s, reach)
    pl.semaphore_wait(barrier, PEERS - 1 + behind + ahead)

    piece = (HEAD // 8, HEAD // 8, width // 4, width // 4, width // 4)
    slab_of = (0, 0, 1, 2, 2)
    slabs = (w_heads, weights.at[0], weights.at[1])
    alls = (None, wq_all, wkv_all)

    def start_of(i, index):
        if slab_of[i] == 0:
            return (index * 2 + i) * piece[i]
        if slab_of[i] == 1:
            return index * piece[i]
        return (2 * y + i - 3) * piece[i]

    def rows_of(i, index):
        return pl.ds(pl.multiple_of(start_of(i, index), 16), piece[i])

    def to_sib(t):
        if t == 0:
            src = w_cut.at[sib]
        else:
            src = alls[t].at[pl.ds(pl.multiple_of(sib * width, 16), width)]
        return remote(C_SIB + t, src, slabs[t].at[SIB], s, sib)

    def to_far(i, slot):
        peer = peers[slot]
        t = slab_of[i]
        if t == 0:
            src = w_cut.at[peer, rows_of(i, quarter)]
        else:
            first = peer * width + start_of(i, quarter)
            src = alls[t].at[pl.ds(pl.multiple_of(first, 16), piece[i])]
        dst = slabs[t].at[slot, rows_of(i, quarter)]
        return remote(C_FAR + 2 * i + slot - ACROSS, src, dst, s, peer)

    def relay(i, slot, step):
        if step < 2:
            index, target = quarter, (pair_z, pair_y)[step]
        elif slab_of[i] == 0 and slot == DIAG:
            index, target = quarter_y, pair_z
        else:
            index, target = quarter_z, pair_y
        block = slabs[slab_of[i]].at[slot, rows_of(i, index)]
        number = 6 * i + 3 * (slot - ACROSS) + step
        return remote(C_RELAY + number, block, block, target, h)

    def steps_of(i):
        return (1,) if slab_of[i] == 2 else (0, 1, 2)

    def relay_first(i):
        for slot in (ACROSS, DIAG):
            to_far(i, slot).wait_recv()
            for step in steps_of(i)[:2]:
                relay(i, slot, step).start()

    def relay_second(i):
        for slot in (ACROSS, DIAG):
            over_y = slab_of[i] == 0 and slot == DIAG
            relay(i, slot, 1 if over_y else 0).wait_recv()
            relay(i, slot, 2).start()

    def arrived(i):
        for slot in (ACROSS, DIAG):
            over_y = slab_of[i] == 0 and slot == DIAG
            relay(i, slot, 0 if over_y else 1).wait_recv()
            if slab_of[i] < 2:
                relay(i, slot, 2).wait_recv()

    for i in (0, 1):
        for slot in (ACROSS, DIAG):
            to_far(i, slot).start()
    to_sib(0).start()
    load_keys.wait()
    load_values.wait()
    halo = [
        remote(C_HALO + d - 1, kv.at[core, reach], kv.at[core, reach - d], s + d, h)
        for d in range(1, reach + 1)
    ]
    passed = [
        remote(C_PASS + d - 1, kv.at[core, reach - d], kv.at[core, reach - d], s, sib)
        for d in range(1, reach + 1)
    ]

    def send_halo(which):
        for d in range(1, reach + 1):
            @pl.when((core == which) & (s + d < seqs))
            def _():
                halo[d - 1].start()

    def pass_halo(which):
        for d in range(1, reach + 1):
            @pl.when((core == which) & (s >= d))
            def _():
                halo[d - 1].wait_recv()
                passed[d - 1].start()

    def get_halo(which):
        for d in range(1, reach + 1):
            @pl.when((core != which) & (s >= d))
            def _():
                passed[d - 1].wait_recv()

    send_halo(0)
    load_dout.wait()
    load_wq.wait()
    load_wk.wait()
    load_own = []
    for t in (1, 2):
        rows_own = pl.ds(pl.multiple_of(h * width, 16), width)
        load_own.append(
            pltpu.make_async_copy(alls[t].at[rows_own], slabs[t].at[0], local.at[6 + t]))
    relay_first(0)
    relay_first(1)
    for slot in (ACROSS, DIAG):
        to_far(2, slot).start()

    to_sib(0).wait_recv()
    rows = tokens // ROW_CHUNKS
    both_heads = 2 * HEAD
    d_all = d_own[...]
    near = w_heads[0:2].reshape(both_heads, wide)
    result = jnp.dot(near, d_all, preferred_element_type=f32).T
    own_part[...] = result[:, :HEAD]
    partial[SIB - 1] = result[:, HEAD:].astype(bf16)
    part = [
        remote(C_PART + r - 1, partial.at[r - 1], partial_in.at[r - 1], s, peers[r])
        for r in range(1, PEERS)
    ]
    part[SIB - 1].start()
    relay_second(0)
    relay_second(1)
    send_halo(1)
    pass_halo(0)
    arrived(0)
    arrived(1)
    far = w_heads[2:4].reshape(both_heads, wide)
    result = jnp.dot(far, d_all, preferred_element_type=f32).T.astype(bf16)
    partial[ACROSS - 1] = result[:, :HEAD]
    partial[DIAG - 1] = result[:, HEAD:]
    part[ACROSS - 1].start()
    part[DIAG - 1].start()
    for copy in load_own:
        copy.start()
    for t in (1, 2):
        to_sib(t).start()
    relay_first(2)
    load_query.wait()
    get_halo(0)

    row = lax.broadcasted_iota(jnp.int32, (tokens, tokens), 0)
    col = lax.broadcasted_iota(jnp.int32, (tokens, tokens), 1)
    query_all = query[...]
    for j in range(reach + 1):
        score = dot_rows(query_all, kv[0, j]) * score_scale
        if j == reach:
            score = jnp.where(col <= row, score, -1e30)
        else:
            score = jnp.where(s >= reach - j, score, -1e30)
            if j == 0:
                score = jnp.where(col > row, score, -1e30)
        probs[:, j * tokens : (j + 1) * tokens] = score
    for i in range(ROW_CHUNKS):
        here = pl.ds(i * rows, rows)
        score = probs[here, :]
        exps = jnp.exp(score - jnp.max(score, axis=1, keepdims=True))
        p = exps * (1.0 / jnp.sum(exps, axis=1, keepdims=True))
        probs[here, :] = p
        low[here, :] = p.astype(bf16)

    pass_halo(1)
    relay_second(2)
    for copy in part:
        copy.wait_recv()
    for i in (3, 4):
        for slot in (ACROSS, DIAG):
            to_far(i, slot).start()
    grad_heads = own_part[...]
    for r in range(1, PEERS):
        grad_heads = grad_heads + partial_in[r - 1].astype(f32)
    grad_heads = grad_heads.astype(bf16)

    swaps = [
        remote(C_SWAP + j, parts.at[1 - core, j], parts_in.at[j], s, sib) for j in range(reach + 1)
    ]

    def start_swap(which, j):
        @pl.when(core == which)
        def _():
            swaps[j].start()

    for j in range(reach + 1):
        parts[1, j] = dot_cols(low[:, j * tokens : (j + 1) * tokens], grad_heads).astype(bf16)
        start_swap(0, j)

    back_copies = [
        remote(C_BACK + d - 1, back.at[reach - d], back_in.at[d - 1], s - d, h)
        for d in range(1, reach + 1)
    ]

    def send_back(which, blocks):
        @pl.when(core == which)
        def _():
            for j in blocks:
                d = reach - j
                swaps[j].wait_recv()
                both = parts[which, j].astype(f32) + parts_in[j].astype(f32)
                if d == 0:
                    total[...] = both
                else:
                    back[j] = both.astype(bf16)

                    @pl.when(s >= d)
                    def _():
                        back_copies[d - 1].start()

    send_back(1, range(2))
    get_halo(1)
    for j in range(reach + 1):
        products[:, j * tokens : (j + 1) * tokens] = dot_rows(grad_heads, kv[1, j])
    send_back(1, range(2, reach + 1))
    for i in range(ROW_CHUNKS):
        here = pl.ds(i * rows, rows)
        p = probs[here, :]
        dp = products[here, :]
        delta = jnp.sum(p * dp, axis=1, keepdims=True)
        ds[here, :] = (p * (dp - delta)).astype(bf16)
    for j in range(reach + 1):
        parts[0, j] = (
            dot_cols(ds[:, j * tokens : (j + 1) * tokens], query[...]) * score_scale
        ).astype(bf16)
        start_swap(1, j)

    grad_query = jnp.zeros((tokens, HEAD), f32)
    for j in range(reach + 1):
        grad_query = grad_query + jnp.dot(
            ds[:, j * tokens : (j + 1) * tokens], kv[0, j], preferred_element_type=f32)
    grads[0, 0] = (grad_query * score_scale).astype(bf16)

    send_back(0, range(reach + 1))

    def share(t):
        return [
            remote(C_GRAD + 3 * t + r - 1, grads.at[t, 0], grads.at[t, r], s, peers[r])
            for r in range(1, PEERS)
        ]

    share_query = share(0)
    for copy in share_query:
        copy.start()
    relay_first(3)

    for copy in share_query:
        copy.wait_recv()
    load_own[0].wait()
    to_sib(1).wait_recv()
    arrived(2)
    chunk = width // 2

    def product(t, slots, first):
        right = jnp.concatenate([grads[t, r] for r in slots], axis=1)
        left = jnp.concatenate([weights[t, r, first : first + chunk] for r in slots], axis=1)
        return dot_rows(left, right)

    for first in range(0, width, chunk):
        acc[first : first + chunk] = product(0, range(PEERS), first)
    relay_first(4)
    for d in range(1, reach + 1):
        @pl.when(s + d < seqs)
        def _():
            back_copies[d - 1].wait_recv()
            total[...] += back_in[d - 1].astype(f32)
    grads[1, 0] = total[...].astype(bf16)
    share_pair = share(1)
    for copy in share_pair:
        copy.start()

    load_own[1].wait()
    to_sib(2).wait_recv()
    share_pair[SIB - 1].wait_recv()
    for first in range(0, width, chunk):
        acc[first : first + chunk] += product(1, (0, SIB), first)
    arrived(3)
    arrived(4)
    for copy in share_pair[SIB:]:
        copy.wait_recv()
    for first in range(0, width, chunk):
        here = slice(first, first + chunk)
        out[here] = (acc[here] + product(1, (ACROSS, DIAG), first)).astype(bf16)

    for copy in part + share_query + share_pair + swaps:
        copy.wait_send()
    for t in range(3):
        to_sib(t).wait_send()
    for i in range(5):
        for slot in (ACROSS, DIAG):
            to_far(i, slot).wait_send()
            for step in steps_of(i):
                relay(i, slot, step).wait_send()
    for d in range(1, reach + 1):
        @pl.when(s + d < seqs)
        def _():
            halo[d - 1].wait_send()

        @pl.when(s >= d)
        def _():
            passed[d - 1].wait_send()
            back_copies[d - 1].wait_send()


def fused(seqs, query, keys, values, d_out, w_out, w_query, w_key, w_value):
    tokens, width = d_out.shape
    wide = -(-width // 128) * 128
    span = (NBR + 1) * tokens
    bf16, f32 = jnp.bfloat16, jnp.float32
    vmem = pl.BlockSpec(memory_space=pltpu.VMEM)
    hbm = pl.BlockSpec(memory_space=pltpu.HBM)
    return pl.pallas_call(
        functools.partial(kernel, seqs),
        out_shape=jax.ShapeDtypeStruct((width, tokens), bf16),
        in_specs=[hbm] * 8,
        out_specs=vmem,
        scratch_shapes=[
            pltpu.VMEM(w_query.shape, bf16),
            pltpu.VMEM(w_key.shape, bf16),
            pltpu.VMEM(w_out.shape, bf16),
            pltpu.VMEM((wide, tokens), bf16),
            pltpu.VMEM((PEERS, HEAD, wide), bf16),
            pltpu.VMEM((PEERS, HEAD, wide), bf16),
            pltpu.VMEM((tokens, HEAD), bf16),
            pltpu.VMEM((2, NBR + 1, tokens, HEAD), bf16),
            pltpu.VMEM((tokens, span), f32),
            pltpu.VMEM((tokens, span), f32),
            pltpu.VMEM((tokens, span), bf16),
            pltpu.VMEM((tokens, span), bf16),
            pltpu.VMEM((tokens, HEAD), f32),
            pltpu.VMEM((PEERS - 1, tokens, HEAD), bf16),
            pltpu.VMEM((PEERS - 1, tokens, HEAD), bf16),
            pltpu.VMEM((2, NBR + 1, tokens, HEAD), bf16),
            pltpu.VMEM((NBR + 1, tokens, HEAD), bf16),
            pltpu.VMEM((NBR, tokens, HEAD), bf16),
            pltpu.VMEM((NBR, tokens, HEAD), bf16),
            pltpu.VMEM((2, PEERS, tokens, HEAD), bf16),
            pltpu.VMEM((2, PEERS, width, HEAD), bf16),
            pltpu.VMEM((tokens, HEAD), f32),
            pltpu.VMEM((width, tokens), f32),
            pltpu.SemaphoreType.DMA((C_END,)),
            pltpu.SemaphoreType.DMA((C_END,)),
            pltpu.SemaphoreType.DMA((9,)),
        ],
        compiler_params=pltpu.CompilerParams(
            collective_id=0, has_side_effects=True, vmem_limit_bytes=48 * 1024 * 1024,
        ),
    )(*(
        pltpu.with_memory_space_constraint(x, pltpu.HBM)
        for x in (query, keys, values, d_out.T, w_out, w_query, w_key, w_value)
    )).T


def solution(mesh):
    in_specs = (
        P("seq", "head"),
        P("seq", "head"),
        P("seq", "head"),
        P("seq", "head"),
        P("head", None),
        P(None, "head"),
        P(None, "head"),
        P(None, "head"),
    )
    out_specs = P("seq", "head")
    seqs, peers = mesh.shape["seq"], mesh.shape["head"]

    def local(query, keys, values, d_out, w_out, w_query, w_key, w_value):
        args = (query, keys, values, d_out, w_out, w_query, w_key, w_value)
        tokens, width = d_out.shape
        fits = peers == PEERS and seqs % 4 == 0 and query.shape[1] == HEAD
        fits = fits and tokens * NBR == WINDOW and width % 64 == 0
        return fused(seqs, *args) if fits else body(*args)

    return jax.shard_map(local, mesh=mesh, in_specs=in_specs, out_specs=out_specs, check_vma=False)
```

```python
import functools

import jax
import jax.numpy as jnp
from jax import lax
from jax.experimental import pallas as pl
from jax.experimental.pallas import tpu as pltpu
from jax.sharding import PartitionSpec as P

WINDOW = 1024
NBR = 4
HEAD = 128


score_scale = 168.0 ** (-0.5)


def from_behind(block, axis, distance):
    devices = range(lax.axis_size(axis))
    route = [(i - distance, i) for i in devices if i - distance in devices]
    return lax.ppermute(block, axis, route)


def dot_rows(left, right):
    return lax.dot_general(
        left, right, (((1,), (1,)), ((), ())), preferred_element_type=jnp.float32
    )


def dot_cols(left, right):
    return lax.dot_general(
        left, right, (((0,), (0,)), ((), ())), preferred_element_type=jnp.float32
    )


def band_backward(query_block, key_band, value_band, grad_block, query_start, key_start):
    length = query_block.shape[0]
    span = key_band.shape[0]
    query_pos = query_start + jnp.arange(length, dtype=jnp.int32)
    key_pos = key_start + jnp.arange(span, dtype=jnp.int32)
    offset = query_pos[:, None] - key_pos[None, :]
    allowed = (key_pos[None, :] >= 0) & (offset >= 0) & (offset < WINDOW)
    scores = dot_rows(query_block, key_band) * score_scale
    masked = jnp.where(allowed, scores, -1e30)
    top = jnp.max(masked, axis=1, keepdims=True)
    weights = jnp.where(allowed, jnp.exp(masked - top), 0.0)
    probs = weights / jnp.sum(weights, axis=1, keepdims=True)
    probs_low = probs.astype(jnp.bfloat16)
    grad_probs = dot_rows(grad_block, value_band)
    delta = jnp.sum(probs * grad_probs, axis=1, keepdims=True)
    grad_scores = (probs * (grad_probs - delta)).astype(jnp.bfloat16)
    grad_query = (
        jnp.dot(grad_scores, key_band, preferred_element_type=jnp.float32) * score_scale
    ).astype(jnp.bfloat16)
    grad_keys = (dot_cols(grad_scores, query_block) * score_scale).astype(jnp.bfloat16)
    grad_values = dot_cols(probs_low, grad_block).astype(jnp.bfloat16)
    return (grad_query, grad_keys, grad_values)


def body(query, keys, values, d_out, w_out, w_query, w_key, w_value):
    length = query.shape[0]
    seq_index = lax.axis_index("seq")
    gathered = lax.all_gather(d_out, "head", axis=1, tiled=True)
    grad_heads = dot_rows(gathered, w_out).astype(jnp.bfloat16)
    reach = NBR
    key_blocks = []
    value_blocks = []
    for distance in range(reach, 0, -1):
        far_keys, far_values = from_behind((keys, values), "seq", distance)
        key_blocks.append(far_keys)
        value_blocks.append(far_values)
    key_band = jnp.concatenate(key_blocks + [keys], axis=0)
    value_band = jnp.concatenate(value_blocks + [values], axis=0)
    query_start = seq_index * length
    grad_query, key_parts, value_parts = band_backward(
        query, key_band, value_band, grad_heads, query_start, query_start - reach * length
    )
    key_total = key_parts[reach * length :].astype(jnp.float32)
    value_total = value_parts[reach * length :].astype(jnp.float32)
    for distance in range(1, reach + 1):
        first = (reach - distance) * length
        outgoing = (key_parts[first : first + length], value_parts[first : first + length])
        back_keys, back_values = from_behind((outgoing[0], outgoing[1]), "seq", -distance)
        key_total = key_total + back_keys.astype(jnp.float32)
        value_total = value_total + back_values.astype(jnp.float32)
    grad_keys = key_total.astype(jnp.bfloat16)
    grad_values = value_total.astype(jnp.bfloat16)
    summed = dot_rows(w_query, grad_query)
    summed = summed + dot_rows(w_key, grad_keys)
    summed = summed + dot_rows(w_value, grad_values)
    reduced = lax.psum_scatter(
        summed.astype(jnp.bfloat16), "head", scatter_dimension=0, tiled=True
    ).astype(jnp.float32)
    return reduced.T.astype(jnp.bfloat16)


PEERS = 4
SIB, ACROSS, DIAG = 1, 2, 3
ROW_CHUNKS = 4
MESH = pl.DeviceIdType.MESH

C_SIB = 0
C_FAR = C_SIB + 3
C_RELAY = C_FAR + 10
C_HALO = C_RELAY + 30
C_PASS = C_HALO + NBR
C_PART = C_PASS + NBR
C_SWAP = C_PART + 3
C_BACK = C_SWAP + 1
C_GRAD = C_BACK + NBR
C_END = C_GRAD + 6


def kernel(
    seqs, query_in, keys_in, values_in, d_out, w_out, w_query, w_key, w_value, out,
    wq_all, wkv_all, wout_all, d_own, w_cut, w_heads, query, kv, probs, products, low, ds,
    own_part, partial, partial_in, parts, parts_in, back, back_in, grads, weights, total, acc,
    send, recv, local,
):
    s = lax.axis_index("seq")
    h = lax.axis_index("head")
    core = lax.rem(h, 2)
    sib = h + 1 - 2 * core
    across = lax.rem(h + 2, 4)
    diag = lax.rem(sib + 2, 4)
    peers = (None, sib, across, diag)
    y = lax.rem(s, 2)
    z = lax.rem(s // 2, 2)
    pair_y = s + 1 - 2 * y
    pair_z = s + 2 - 4 * z
    quarter = 2 * y + z
    quarter_z = 2 * y + 1 - z
    quarter_y = 2 - 2 * y + z
    width, tokens = out.shape
    wide = d_own.shape[0]
    reach = NBR
    f32, bf16 = jnp.float32, jnp.bfloat16

    barrier = pltpu.get_barrier_semaphore()
    for r in range(1, PEERS):
        pl.semaphore_signal(barrier, inc=1, device_id=(s, peers[r]), device_id_type=MESH)
    for d in range(1, reach + 1):
        @pl.when(s >= d)
        def _():
            pl.semaphore_signal(barrier, inc=1, device_id=(s - d, h), device_id_type=MESH)

        @pl.when(s + d < seqs)
        def _():
            pl.semaphore_signal(barrier, inc=1, device_id=(s + d, h), device_id_type=MESH)

    def remote(index, src, dst, seq, head):
        return pltpu.make_async_remote_copy(
            src_ref=src, dst_ref=dst, send_sem=send.at[index], recv_sem=recv.at[index],
            device_id=(seq, head), device_id_type=MESH,
        )

    load_wout = pltpu.make_async_copy(w_out, wout_all, local.at[0])
    load_dout = pltpu.make_async_copy(d_out, d_own.at[pl.ds(0, width)], local.at[1])
    load_keys = pltpu.make_async_copy(keys_in, kv.at[0, reach], local.at[2])
    load_values = pltpu.make_async_copy(values_in, kv.at[1, reach], local.at[3])
    load_query = pltpu.make_async_copy(query_in, query, local.at[4])
    load_wq = pltpu.make_async_copy(w_query, wq_all, local.at[5])
    load_wk = pltpu.make_async_copy(w_key, wkv_all, local.at[6])
    load_wv = pltpu.make_async_copy(w_value, wkv_all, local.at[6])
    for copy in (load_wout, load_keys, load_values, load_dout, load_query):
        copy.start()

    for d in range(1, reach + 1):
        @pl.when(s < d)
        def _():
            kv[0, reach - d] = jnp.zeros((tokens, HEAD), bf16)
            kv[1, reach - d] = jnp.zeros((tokens, HEAD), bf16)

    d_own[width:wide] = jnp.zeros((wide - width, tokens), bf16)

    pad = jnp.zeros((HEAD, wide - width), bf16)
    load_wout.wait()
    load_wq.start()

    @pl.when(core == 0)
    def _():
        load_wk.start()

    @pl.when(core == 1)
    def _():
        load_wv.start()

    for b in range(PEERS):
        shift = b * width % 128
        first = b * width - shift
        room = min(width + 128, wout_all.shape[1] - first)
        cut = wout_all[:, first : first + room][:, shift : shift + width]
        cut = jnp.concatenate([cut, pad], axis=1)
        w_cut[b] = cut

        @pl.when(h == b)
        def _():
            w_heads[0] = cut

    behind = jnp.minimum(s, reach)
    ahead = jnp.minimum(seqs - 1 - s, reach)
    pl.semaphore_wait(barrier, PEERS - 1 + behind + ahead)

    piece = (HEAD // 8, HEAD // 8, width // 4, width // 4, width // 4)
    slab_of = (0, 0, 1, 2, 2)
    slabs = (w_heads, weights.at[0], weights.at[1])
    alls = (None, wq_all, wkv_all)

    def start_of(i, index):
        if slab_of[i] == 0:
            return (index * 2 + i) * piece[i]
        if slab_of[i] == 1:
            return index * piece[i]
        return (2 * y + i - 3) * piece[i]

    def rows_of(i, index):
        return pl.ds(pl.multiple_of(start_of(i, index), 16), piece[i])

    def to_sib(t):
        if t == 0:
            src = w_cut.at[sib]
        else:
            src = alls[t].at[pl.ds(pl.multiple_of(sib * width, 16), width)]
        return remote(C_SIB + t, src, slabs[t].at[SIB], s, sib)

    def to_far(i, slot):
        peer = peers[slot]
        t = slab_of[i]
        if t == 0:
            src = w_cut.at[peer, rows_of(i, quarter)]
        else:
            first = peer * width + start_of(i, quarter)
            src = alls[t].at[pl.ds(pl.multiple_of(first, 16), piece[i])]
        dst = slabs[t].at[slot, rows_of(i, quarter)]
        return remote(C_FAR + 2 * i + slot - ACROSS, src, dst, s, peer)

    def relay(i, slot, step):
        if step < 2:
            index, target = quarter, (pair_z, pair_y)[step]
        elif slab_of[i] == 0 and slot == DIAG:
            index, target = quarter_y, pair_z
        else:
            index, target = quarter_z, pair_y
        block = slabs[slab_of[i]].at[slot, rows_of(i, index)]
        number = 6 * i + 3 * (slot - ACROSS) + step
        return remote(C_RELAY + number, block, block, target, h)

    def steps_of(i):
        return (1,) if slab_of[i] == 2 else (0, 1, 2)

    def relay_first(i):
        for slot in (ACROSS, DIAG):
            to_far(i, slot).wait_recv()
            for step in steps_of(i)[:2]:
                relay(i, slot, step).start()

    def relay_second(i):
        for slot in (ACROSS, DIAG):
            over_y = slab_of[i] == 0 and slot == DIAG
            relay(i, slot, 1 if over_y else 0).wait_recv()
            relay(i, slot, 2).start()

    def arrived(i):
        for slot in (ACROSS, DIAG):
            over_y = slab_of[i] == 0 and slot == DIAG
            relay(i, slot, 0 if over_y else 1).wait_recv()
            if slab_of[i] < 2:
                relay(i, slot, 2).wait_recv()

    for i in (0, 1):
        for slot in (ACROSS, DIAG):
            to_far(i, slot).start()
    to_sib(0).start()
    load_keys.wait()
    load_values.wait()
    halo = [
        remote(C_HALO + d - 1, kv.at[core, reach], kv.at[core, reach - d], s + d, h)
        for d in range(1, reach + 1)
    ]
    passed = [
        remote(C_PASS + d - 1, kv.at[core, reach - d], kv.at[core, reach - d], s, sib)
        for d in range(1, reach + 1)
    ]

    def send_halo(which):
        for d in range(1, reach + 1):
            @pl.when((core == which) & (s + d < seqs))
            def _():
                halo[d - 1].start()

    def pass_halo(which):
        for d in range(1, reach + 1):
            @pl.when((core == which) & (s >= d))
            def _():
                halo[d - 1].wait_recv()
                passed[d - 1].start()

    def get_halo(which):
        for d in range(1, reach + 1):
            @pl.when((core != which) & (s >= d))
            def _():
                passed[d - 1].wait_recv()

    send_halo(0)
    load_dout.wait()
    load_wq.wait()
    load_wk.wait()
    load_own = []
    for t in (1, 2):
        rows_own = pl.ds(pl.multiple_of(h * width, 16), width)
        load_own.append(
            pltpu.make_async_copy(alls[t].at[rows_own], slabs[t].at[0], local.at[6 + t]))
    relay_first(0)
    relay_first(1)
    for i in (2, 3, 4):
        for slot in (ACROSS, DIAG):
            to_far(i, slot).start()

    to_sib(0).wait_recv()
    rows = tokens // ROW_CHUNKS
    both_heads = 2 * HEAD
    d_all = d_own[...]
    near = w_heads[0:2].reshape(both_heads, wide)
    result = jnp.dot(near, d_all, preferred_element_type=f32).T
    own_part[...] = result[:, :HEAD]
    partial[SIB - 1] = result[:, HEAD:].astype(bf16)
    part = [
        remote(C_PART + r - 1, partial.at[r - 1], partial_in.at[r - 1], s, peers[r])
        for r in range(1, PEERS)
    ]
    part[SIB - 1].start()
    relay_second(0)
    relay_second(1)
    send_halo(1)
    pass_halo(0)
    arrived(0)
    arrived(1)
    far = w_heads[2:4].reshape(both_heads, wide)
    result = jnp.dot(far, d_all, preferred_element_type=f32).T.astype(bf16)
    partial[ACROSS - 1] = result[:, :HEAD]
    partial[DIAG - 1] = result[:, HEAD:]
    part[ACROSS - 1].start()
    part[DIAG - 1].start()
    for copy in load_own:
        copy.start()
    for t in (1, 2):
        to_sib(t).start()
    relay_first(2)
    load_query.wait()
    get_halo(0)

    row = lax.broadcasted_iota(jnp.int32, (tokens, tokens), 0)
    col = lax.broadcasted_iota(jnp.int32, (tokens, tokens), 1)
    query_all = query[...]
    for j in range(reach + 1):
        score = dot_rows(query_all, kv[0, j]) * score_scale
        if j == reach:
            score = jnp.where(col <= row, score, -1e30)
        else:
            score = jnp.where(s >= reach - j, score, -1e30)
            if j == 0:
                score = jnp.where(col > row, score, -1e30)
        probs[:, j * tokens : (j + 1) * tokens] = score
    for i in range(ROW_CHUNKS):
        here = pl.ds(i * rows, rows)
        score = probs[here, :]
        exps = jnp.exp(score - jnp.max(score, axis=1, keepdims=True))
        p = exps * (1.0 / jnp.sum(exps, axis=1, keepdims=True))
        probs[here, :] = p
        low[here, :] = p.astype(bf16)

    pass_halo(1)
    relay_second(2)
    for copy in part:
        copy.wait_recv()
    relay_first(3)
    grad_heads = own_part[...]
    for r in range(1, PEERS):
        grad_heads = grad_heads + partial_in[r - 1].astype(f32)
    grad_heads = grad_heads.astype(bf16)

    for j in range(reach + 1):
        parts[1, j] = dot_cols(low[:, j * tokens : (j + 1) * tokens], grad_heads).astype(bf16)
    swap = remote(C_SWAP, parts.at[1 - core], parts_in, s, sib)

    @pl.when(core == 0)
    def _():
        swap.start()

    back_copies = [
        remote(C_BACK + d - 1, back.at[reach - d], back_in.at[d - 1], s - d, h)
        for d in range(1, reach + 1)
    ]

    def send_back(which):
        @pl.when(core == which)
        def _():
            swap.wait_recv()
            for d in range(reach, -1, -1):
                j = reach - d
                both = parts[which, j].astype(f32) + parts_in[j].astype(f32)
                if d == 0:
                    total[...] = both
                else:
                    back[j] = both.astype(bf16)

                    @pl.when(s >= d)
                    def _():
                        back_copies[d - 1].start()

    get_halo(1)
    for j in range(reach + 1):
        products[:, j * tokens : (j + 1) * tokens] = dot_rows(grad_heads, kv[1, j])
    send_back(1)
    for i in range(ROW_CHUNKS):
        here = pl.ds(i * rows, rows)
        p = probs[here, :]
        dp = products[here, :]
        delta = jnp.sum(p * dp, axis=1, keepdims=True)
        ds[here, :] = (p * (dp - delta)).astype(bf16)
    for j in range(reach + 1):
        parts[0, j] = (
            dot_cols(ds[:, j * tokens : (j + 1) * tokens], query[...]) * score_scale
        ).astype(bf16)

    @pl.when(core == 1)
    def _():
        swap.start()

    grad_query = jnp.zeros((tokens, HEAD), f32)
    for j in range(reach + 1):
        grad_query = grad_query + jnp.dot(
            ds[:, j * tokens : (j + 1) * tokens], kv[0, j], preferred_element_type=f32)
    grads[0, 0] = (grad_query * score_scale).astype(bf16)

    send_back(0)

    def share(t):
        return [
            remote(C_GRAD + 3 * t + r - 1, grads.at[t, 0], grads.at[t, r], s, peers[r])
            for r in range(1, PEERS)
        ]

    share_query = share(0)
    for copy in share_query:
        copy.start()
    relay_first(4)

    for copy in share_query:
        copy.wait_recv()
    load_own[0].wait()
    to_sib(1).wait_recv()
    arrived(2)
    chunk = width // 2

    def product(t, slots, first):
        right = jnp.concatenate([grads[t, r] for r in slots], axis=1)
        left = jnp.concatenate([weights[t, r, first : first + chunk] for r in slots], axis=1)
        return dot_rows(left, right)

    for first in range(0, width, chunk):
        acc[first : first + chunk] = product(0, range(PEERS), first)
    for d in range(1, reach + 1):
        @pl.when(s + d < seqs)
        def _():
            back_copies[d - 1].wait_recv()
            total[...] += back_in[d - 1].astype(f32)
    grads[1, 0] = total[...].astype(bf16)
    share_pair = share(1)
    for copy in share_pair:
        copy.start()

    load_own[1].wait()
    to_sib(2).wait_recv()
    share_pair[SIB - 1].wait_recv()
    for first in range(0, width, chunk):
        acc[first : first + chunk] += product(1, (0, SIB), first)
    arrived(3)
    arrived(4)
    for copy in share_pair[SIB:]:
        copy.wait_recv()
    for first in range(0, width, chunk):
        here = slice(first, first + chunk)
        out[here] = (acc[here] + product(1, (ACROSS, DIAG), first)).astype(bf16)

    for copy in part + share_query + share_pair + [swap]:
        copy.wait_send()
    for t in range(3):
        to_sib(t).wait_send()
    for i in range(5):
        for slot in (ACROSS, DIAG):
            to_far(i, slot).wait_send()
            for step in steps_of(i):
                relay(i, slot, step).wait_send()
    for d in range(1, reach + 1):
        @pl.when(s + d < seqs)
        def _():
            halo[d - 1].wait_send()

        @pl.when(s >= d)
        def _():
            passed[d - 1].wait_send()
            back_copies[d - 1].wait_send()


def fused(seqs, query, keys, values, d_out, w_out, w_query, w_key, w_value):
    tokens, width = d_out.shape
    wide = -(-width // 128) * 128
    span = (NBR + 1) * tokens
    bf16, f32 = jnp.bfloat16, jnp.float32
    vmem = pl.BlockSpec(memory_space=pltpu.VMEM)
    hbm = pl.BlockSpec(memory_space=pltpu.HBM)
    return pl.pallas_call(
        functools.partial(kernel, seqs),
        out_shape=jax.ShapeDtypeStruct((width, tokens), bf16),
        in_specs=[hbm] * 8,
        out_specs=vmem,
        scratch_shapes=[
            pltpu.VMEM(w_query.shape, bf16),
            pltpu.VMEM(w_key.shape, bf16),
            pltpu.VMEM(w_out.shape, bf16),
            pltpu.VMEM((wide, tokens), bf16),
            pltpu.VMEM((PEERS, HEAD, wide), bf16),
            pltpu.VMEM((PEERS, HEAD, wide), bf16),
            pltpu.VMEM((tokens, HEAD), bf16),
            pltpu.VMEM((2, NBR + 1, tokens, HEAD), bf16),
            pltpu.VMEM((tokens, span), f32),
            pltpu.VMEM((tokens, span), f32),
            pltpu.VMEM((tokens, span), bf16),
            pltpu.VMEM((tokens, span), bf16),
            pltpu.VMEM((tokens, HEAD), f32),
            pltpu.VMEM((PEERS - 1, tokens, HEAD), bf16),
            pltpu.VMEM((PEERS - 1, tokens, HEAD), bf16),
            pltpu.VMEM((2, NBR + 1, tokens, HEAD), bf16),
            pltpu.VMEM((NBR + 1, tokens, HEAD), bf16),
            pltpu.VMEM((NBR, tokens, HEAD), bf16),
            pltpu.VMEM((NBR, tokens, HEAD), bf16),
            pltpu.VMEM((2, PEERS, tokens, HEAD), bf16),
            pltpu.VMEM((2, PEERS, width, HEAD), bf16),
            pltpu.VMEM((tokens, HEAD), f32),
            pltpu.VMEM((width, tokens), f32),
            pltpu.SemaphoreType.DMA((C_END,)),
            pltpu.SemaphoreType.DMA((C_END,)),
            pltpu.SemaphoreType.DMA((9,)),
        ],
        compiler_params=pltpu.CompilerParams(
            collective_id=0, has_side_effects=True, vmem_limit_bytes=48 * 1024 * 1024,
        ),
    )(*(
        pltpu.with_memory_space_constraint(x, pltpu.HBM)
        for x in (query, keys, values, d_out.T, w_out, w_query, w_key, w_value)
    )).T


def solution(mesh):
    in_specs = (
        P("seq", "head"),
        P("seq", "head"),
        P("seq", "head"),
        P("seq", "head"),
        P("head", None),
        P(None, "head"),
        P(None, "head"),
        P(None, "head"),
    )
    out_specs = P("seq", "head")
    seqs, peers = mesh.shape["seq"], mesh.shape["head"]

    def local(query, keys, values, d_out, w_out, w_query, w_key, w_value):
        args = (query, keys, values, d_out, w_out, w_query, w_key, w_value)
        tokens, width = d_out.shape
        fits = peers == PEERS and seqs % 4 == 0 and query.shape[1] == HEAD
        fits = fits and tokens * NBR == WINDOW and width % 64 == 0
        return fused(seqs, *args) if fits else body(*args)

    return jax.shard_map(local, mesh=mesh, in_specs=in_specs, out_specs=out_specs, check_vma=False)
```
